32 devices in a mesh: expert: 8 (over y, x, core), dp: 4 (over z).
Axes of the slice: x: 2, y: 2, z: 4, core: 2. Of those that a mesh axis runs over, the one named last changes fastest.
Arguments:
- tokens: bfloat16 [4096, 1024], P(('expert', 'dp')), may hold values from -6 to 6
- expert_ids: int32 [4096, 2], P(('expert', 'dp')), may hold values from 0 to 7, as said below
- slot_index: int32 [4096, 2], P(('expert', 'dp')), may hold values from 0 to 39, as said below
- keep_mask: int32 [4096, 2], P(('expert', 'dp')), may hold values from 0 to 1, as said below
- route_weight: float32 [4096, 2], P(('expert', 'dp')), may hold values from 0.2 to 1
- cotangent: bfloat16 [4096, 1024], P(('expert', 'dp')), may hold values from -6 to 6
- w_gate: bfloat16 [8, 1024, 768], P('expert'), may hold values from -0.1875 to 0.1875
- w_up: bfloat16 [8, 1024, 768], P('expert'), may hold values from -0.1875 to 0.1875
- w_down: bfloat16 [8, 768, 1024], P('expert'), may hold values from -0.21875 to 0.21875
Outputs:
- layer_output: bfloat16 [4096, 1024], P(('expert', 'dp'))
- route_grad: float32 [4096, 2], P(('expert', 'dp'))
- input_grad: bfloat16 [4096, 1024], P(('expert', 'dp'))
- gate_grad: float32 [8, 1024, 768], P('expert', None, 'dp')
- up_grad: float32 [8, 1024, 768], P('expert', None, 'dp')
- down_grad: float32 [8, 768, 1024], P('expert', 'dp')
The draws below stay inside these ranges and needn't reach their ends.
Inputs may be any that keep to these rules, and one draw needn't show every extreme that they name: `expert_ids`: the two experts of a token differ. In every index of dp, one expert gets 40 or more routes from every device of that index, and it differs from index to index as drawn. `slot_index`: A route's slot is its rank among the routes of its device's block of 128 tokens to the same expert, counted token by token with the first route before the second; routes of rank 40 or more have slot 39. `keep_mask`: A route is kept exactly when its rank is under 40, so kept routes of one block to one expert have distinct slots, and in every block some expert has all 40 slots kept.
All inputs are finite; a program needn't handle non-finite values.
Results may differ from the reference program's by a relative error of at most 0.0085.
Values may be sent and summed in bfloat16 or wider, within the bound.
A program may use at most 64 MiB of HBM per device.

```python
import math
import jax
import jax.numpy as jnp
from jax import lax

D = 1024
H = 768
TOK_DEV = 128
EXPERTS = 8
CAP = 40
TOKENS = 4096
N_EXPERT = 8
N_DP = 4


def route_table(key):
    blocks = TOKENS // TOK_DEV
    keys = jax.random.split(key, 4)
    hot_group = jax.random.randint(keys[0], (N_DP,), 0, EXPERTS)
    hot_block = jnp.tile(hot_group, blocks // N_DP)
    orders = jax.vmap(lambda single: jax.random.permutation(single, TOK_DEV))(jax.random.split(keys[1], blocks))
    chosen = jax.random.randint(keys[2], (blocks, TOK_DEV), 0, EXPERTS)
    first_route = jnp.where(orders < TOK_DEV // 2, hot_block[:, None], chosen)
    offset = jax.random.randint(keys[3], (blocks, TOK_DEV), 1, EXPERTS)
    second_route = (first_route + offset) % EXPERTS
    routes = jnp.stack([first_route, second_route], axis=-1).reshape(blocks, 2 * TOK_DEV)
    onehot = (routes[..., None] == jnp.arange(EXPERTS, dtype=jnp.int32)).astype(jnp.int32)
    earlier = jnp.cumsum(onehot, axis=1) - onehot
    ranks = jnp.sum(earlier * onehot, axis=-1)
    return (routes.reshape(TOKENS, 2).astype(jnp.int32), ranks.reshape(TOKENS, 2).astype(jnp.int32))


def draw_expert_ids(key, part):
    routes, ranks = route_table(key)
    return routes


def draw_slot_index(key, part):
    routes, ranks = route_table(key)
    return jnp.minimum(ranks, CAP - 1).astype(jnp.int32)


def draw_keep_mask(key, part):
    routes, ranks = route_table(key)
    return (ranks < CAP).astype(jnp.int32)


def block_scale(key, extent, cuts, smallest, top_value):
    def one(position, blocks):
        draws = jax.random.uniform(jax.random.fold_in(jax.random.fold_in(key, 6), position), (blocks,), jnp.float32, smallest / len(cuts), top_value / len(cuts))
        return jnp.repeat(jnp.exp(draws), extent[position] // blocks).reshape((-1,) + (1,) * (len(extent) - position - 1))

    gain = one(*cuts[0])
    for cut in cuts[1:]:
        gain = gain * one(*cut)
    return gain


def gaussian(stream_key, shape, deviation, most, cuts=(), held_as=jnp.bfloat16):
    values = jax.random.normal(stream_key, shape, jnp.float32) * deviation
    if len(cuts) > 0:
        values = block_scale(stream_key, shape, cuts, -0.22, 0.18) * values
    return jnp.clip(values, min=-most, max=most).astype(held_as)


def setup_inputs(seed: int = 0) -> dict:
    key_of = jax.random.split(jax.random.key(seed), 10)
    tokens = gaussian(key_of[0], (TOKENS, D), 1.0, 6.0, ((0, 32),))
    expert_ids = draw_expert_ids(jax.random.fold_in(key_of[9], 71), 0)
    slot_index = draw_slot_index(jax.random.fold_in(key_of[9], 71), 0)
    keep_mask = draw_keep_mask(jax.random.fold_in(key_of[9], 71), 0)
    route_weight = jnp.clip(jnp.exp(math.log(1.0) - 1.609438 * jax.random.uniform(key_of[4], (TOKENS, 2), jnp.float32) ** block_scale(key_of[4], (TOKENS, 2), ((0, 32),), -0.2, 0.2)), 0.2, 1.0)
    cotangent = gaussian(key_of[5], (TOKENS, D), 1.0, 6.0, ((0, 32),))
    w_gate = gaussian(key_of[6], (EXPERTS, D, H), D ** -0.5, 0.1875, ((0, 8),))
    w_up = gaussian(key_of[7], (EXPERTS, D, H), D ** -0.5, 0.1875, ((0, 8),))
    w_down = gaussian(key_of[8], (EXPERTS, H, D), H ** -0.5, 0.21875, ((0, 8),))
    return dict(tokens=tokens, expert_ids=expert_ids, slot_index=slot_index, keep_mask=keep_mask, route_weight=route_weight, cotangent=cotangent, w_gate=w_gate, w_up=w_up, w_down=w_down)


def rounded(value):
    return lax.optimization_barrier(value.astype(jnp.bfloat16)).astype(jnp.float32)


def route_matrix(route_ids, route_slots, route_keep):
    flat_index = route_ids * CAP + route_slots
    cells = jnp.arange(EXPERTS * CAP, dtype=jnp.int32)
    return ((flat_index[..., None] == cells) & (route_keep[..., None] == 1)).astype(jnp.float32)


def regroup(array):
    shaped = array.reshape((N_EXPERT, N_DP, TOK_DEV) + array.shape[1:])
    return jnp.swapaxes(shaped, 0, 1)


def ungroup(array):
    return jnp.swapaxes(array, 0, 1).reshape((TOKENS,) + array.shape[3:])


def to_experts(array):
    return jnp.swapaxes(array.reshape(N_EXPERT, EXPERTS, CAP, D), 0, 1).reshape(EXPERTS, N_EXPERT * CAP, D)


def to_sources(array):
    return jnp.swapaxes(array.reshape(EXPERTS, N_EXPERT, CAP, D), 0, 1).reshape(N_EXPERT, EXPERTS * CAP, D)


def reference(tokens, expert_ids, slot_index, keep_mask, route_weight, cotangent, w_gate, w_up, w_down):
    gate_full = w_gate.astype(jnp.float32)
    up_full = w_up.astype(jnp.float32)
    down_full = w_down.astype(jnp.float32)

    def group_step(totals, group):
        inputs, route_ids, route_slots, route_keep, weights, out_grad = group
        matrix = route_matrix(route_ids, route_slots, route_keep)
        sent_x = jnp.einsum('stkc,std->scd', matrix, inputs.astype(jnp.float32))
        scaled = rounded(weights[..., None] * out_grad[:, :, None, :].astype(jnp.float32))
        sent_g = jnp.einsum('stkc,stkd->scd', matrix, scaled)
        rows_in = to_experts(sent_x)
        rows_grad = to_experts(sent_g)
        gate_value = jnp.einsum('erd,edh->erh', rows_in, gate_full)
        up_value = jnp.einsum('erd,edh->erh', rows_in, up_full)
        sigmoid_gate = jax.nn.sigmoid(gate_value)
        activation = rounded(gate_value * sigmoid_gate * up_value)
        expert_out = rounded(jnp.einsum('erh,ehd->erd', activation, down_full))
        act_grad = jnp.einsum('erd,ehd->erh', rows_grad, down_full)
        up_value_grad = rounded(act_grad * gate_value * sigmoid_gate)
        gate_value_grad = rounded(act_grad * up_value * sigmoid_gate * (1.0 + gate_value * (1.0 - sigmoid_gate)))
        row_input_grad = rounded(jnp.einsum('erh,edh->erd', gate_value_grad, gate_full)
                                 + jnp.einsum('erh,edh->erd', up_value_grad, up_full))
        part_gate = rounded(jnp.einsum('erd,erh->edh', rows_in, gate_value_grad))
        part_up = rounded(jnp.einsum('erd,erh->edh', rows_in, up_value_grad))
        part_down = rounded(jnp.einsum('erh,erd->ehd', activation, rows_grad))
        back_out = to_sources(expert_out)
        back_grad = to_sources(row_input_grad)
        picked = jnp.einsum('stkc,scd->stkd', matrix, back_out)
        layer_output = jnp.sum(weights[..., None] * picked, axis=2).astype(jnp.bfloat16)
        route_grad = jnp.sum(out_grad.astype(jnp.float32)[:, :, None, :] * picked, axis=3)
        input_grad = jnp.einsum('stkc,scd->std', matrix, back_grad).astype(jnp.bfloat16)
        totals = (totals[0] + part_gate, totals[1] + part_up, totals[2] + part_down)
        return totals, (layer_output, route_grad, input_grad)

    start = (jnp.zeros((EXPERTS, D, H), jnp.float32), jnp.zeros((EXPERTS, D, H), jnp.float32),
             jnp.zeros((EXPERTS, H, D), jnp.float32))
    groups = (regroup(tokens), regroup(expert_ids), regroup(slot_index), regroup(keep_mask),
              regroup(route_weight), regroup(cotangent))
    totals, results = lax.scan(group_step, start, groups)
    layer_output = ungroup(results[0])
    route_grad = ungroup(results[1])
    input_grad = ungroup(results[2])
    return (layer_output, route_grad, input_grad,
            totals[0] / N_DP, totals[1] / N_DP, totals[2] / N_DP)
```

```python
import functools

import jax
import jax.numpy as jnp
from jax import lax
from jax.experimental import pallas as pl
from jax.experimental.pallas import tpu as pltpu
from jax.sharding import PartitionSpec as P

MESH = pl.DeviceIdType.MESH


def expert_forward(rows_in, gate_mat, up_mat, down_mat):
    gate_value = jnp.dot(rows_in, gate_mat, preferred_element_type=jnp.float32)
    up_value = jnp.dot(rows_in, up_mat, preferred_element_type=jnp.float32)
    sigmoid_gate = jax.nn.sigmoid(gate_value)
    activation = (gate_value * sigmoid_gate * up_value).astype(jnp.bfloat16)
    expert_out = jnp.dot(activation, down_mat, preferred_element_type=jnp.float32).astype(
        jnp.bfloat16
    )
    return (gate_value, up_value, sigmoid_gate, activation, expert_out)


def value_grads(rows_grad, down_mat, gate_value, up_value, sigmoid_gate):
    act_grad = lax.dot_general(
        rows_grad, down_mat, (((1,), (1,)), ((), ())), preferred_element_type=jnp.float32
    )
    up_value_grad = (act_grad * gate_value * sigmoid_gate).astype(jnp.bfloat16)
    gate_value_grad = (
        act_grad * up_value * sigmoid_gate * (1.0 + gate_value * (1.0 - sigmoid_gate))
    ).astype(jnp.bfloat16)
    return (gate_value_grad, up_value_grad)


def column_product(left, right):
    return lax.dot_general(
        left, right, (((0,), (0,)), ((), ())), preferred_element_type=jnp.float32
    )


def body(tokens, expert_ids, slot_index, keep_mask, route_weight, cotangent, w_gate, w_up, w_down):
    groups = lax.axis_size("expert")
    data_groups = lax.axis_size("dp")
    local_tokens = tokens.shape[0]
    width = tokens.shape[1]
    experts_all = groups * w_gate.shape[0]
    capacity = 5 * local_tokens // (2 * experts_all)
    gate_mat = w_gate[0]
    up_mat = w_up[0]
    down_mat = w_down[0]
    flat_index = expert_ids * capacity + slot_index
    cells = jnp.arange(experts_all * capacity, dtype=jnp.int32)
    matrix = ((flat_index[..., None] == cells) & (keep_mask[..., None] == 1)).astype(jnp.bfloat16)
    send_in = jnp.einsum("tkc,td->cd", matrix, tokens, preferred_element_type=jnp.float32)
    send_in = send_in.astype(jnp.bfloat16).reshape(experts_all, capacity, width)
    scaled = (route_weight[..., None] * cotangent[:, None, :].astype(jnp.float32)).astype(
        jnp.bfloat16
    )
    send_grad = jnp.einsum("tkc,tkd->cd", matrix, scaled, preferred_element_type=jnp.float32)
    send_grad = send_grad.astype(jnp.bfloat16).reshape(experts_all, capacity, width)
    rows_in = lax.all_to_all(send_in, "expert", split_axis=0, concat_axis=0, tiled=True)
    rows_in = rows_in.reshape(-1, width)
    gate_value, up_value, sigmoid_gate, activation, expert_out = expert_forward(
        rows_in, gate_mat, up_mat, down_mat
    )
    out_blocks = expert_out.reshape(groups, capacity, width)
    back_out = lax.all_to_all(out_blocks, "expert", split_axis=0, concat_axis=0, tiled=True)
    rows_grad = lax.all_to_all(
        send_grad, "expert", split_axis=0, concat_axis=0, tiled=True
    ).reshape(-1, width)
    part_down = column_product(activation, rows_grad)
    gate_value_grad, up_value_grad = value_grads(
        rows_grad, down_mat, gate_value, up_value, sigmoid_gate
    )
    part_gate = column_product(rows_in, gate_value_grad)
    part_up = column_product(rows_in, up_value_grad)
    gate_sum, up_sum, down_sum = (
        lax.psum_scatter(
            part_gate.astype(jnp.bfloat16), "dp", scatter_dimension=1, tiled=True
        ).astype(jnp.float32),
        lax.psum_scatter(
            part_up.astype(jnp.bfloat16), "dp", scatter_dimension=1, tiled=True
        ).astype(jnp.float32),
        lax.psum_scatter(
            part_down.astype(jnp.bfloat16), "dp", scatter_dimension=0, tiled=True
        ).astype(jnp.float32),
    )
    row_input_grad = lax.dot_general(
        gate_value_grad, gate_mat, (((1,), (1,)), ((), ())), preferred_element_type=jnp.float32
    ) + lax.dot_general(
        up_value_grad, up_mat, (((1,), (1,)), ((), ())), preferred_element_type=jnp.float32
    )
    grad_blocks = row_input_grad.astype(jnp.bfloat16).reshape(groups, capacity, width)
    back_grad = lax.all_to_all(grad_blocks, "expert", split_axis=0, concat_axis=0, tiled=True)
    back_out = back_out.reshape(-1, width)
    back_grad = back_grad.reshape(-1, width)
    picked = jnp.einsum("tkc,cd->tkd", matrix, back_out, preferred_element_type=jnp.float32)
    layer_output = jnp.sum(route_weight[..., None] * picked, axis=1).astype(jnp.bfloat16)
    route_grad = jnp.einsum(
        "td,tkd->tk", cotangent, picked.astype(jnp.bfloat16), preferred_element_type=jnp.float32
    )
    input_grad = jnp.einsum(
        "tkc,cd->td", matrix, back_grad, preferred_element_type=jnp.float32
    ).astype(jnp.bfloat16)
    scale = 1.0 / data_groups
    return (
        layer_output,
        route_grad,
        input_grad,
        (gate_sum * scale)[None],
        (up_sum * scale)[None],
        (down_sum * scale)[None],
    )


def dot(left, right, left_dim=1, right_dim=0):
    return lax.dot_general(
        left, right, (((left_dim,), (right_dim,)), ((), ())), preferred_element_type=jnp.float32
    )


def group_order(index):
    half = index // 2
    side = (1 - half) * index + half * (3 - index)
    order = []
    for step, swapped in enumerate((1, 0, 2, 3)):
        place = (1 - side) * step + side * swapped
        order.append((1 - half) * place + half * (3 - place))
    return order


def kernel(
    n, capacity, share,
    tok_ref, cot_ref, meta_ref, index_ref, weight_ref, wg_ref, wu_ref, wd_ref, wgu_s_ref, wd_s_ref,
    out_ref, route_ref, input_ref, gate_ref, up_ref, down_ref,
    ztok, zcot, zmeta, send, recv, back_send, back_recv, out_acc, rig_acc,
    z_send_sem, z_recv_sem, x_send_sem, x_recv_sem, b_send_sem, b_recv_sem, own_sem,
):
    me = lax.axis_index("expert")
    group = lax.axis_index("dp")
    order = group_order(group)
    width = tok_ref.shape[1]
    pair = 2 * capacity
    cells = n * pair
    hidden = wg_ref.shape[1]
    tile = 256
    peers = [lax.rem(me + step, n) for step in range(1, n)]

    def dispatch(step, tok, cot, meta):
        first, second = meta[0:1, :], meta[1:2, :]
        w_first, w_second = meta[2:3, :], meta[3:4, :]
        cell = lax.broadcasted_iota(jnp.int32, (cells, tok.shape[0]), 0).astype(jnp.float32)
        to_tok = jnp.where((cell == first) | (cell == second), 1.0, 0.0)
        low = cell - capacity
        hit_first, hit_second = low == first, low == second
        to_cot = jnp.where(hit_first | hit_second, 1.0, 0.0)
        weight = jnp.where(hit_first, w_first, 0.0) + jnp.where(hit_second, w_second, 0.0)
        weight = jnp.sum(weight + to_tok, axis=1, keepdims=True)
        picked = dot(to_tok.astype(jnp.bfloat16), tok) + dot(to_cot.astype(jnp.bfloat16), cot)
        send[step] = (picked * weight).astype(jnp.bfloat16).reshape(n, pair, width)

    def x_copy(step, slot, peer):
        return pltpu.make_async_remote_copy(
            src_ref=send.at[step, peer], dst_ref=recv.at[step, slot],
            send_sem=x_send_sem.at[step, peer], recv_sem=x_recv_sem.at[step, slot],
            device_id=(peer, group), device_id_type=MESH,
        )

    def own_copy(step):
        return pltpu.make_async_copy(send.at[step, me], recv.at[step, me], own_sem.at[step])

    def x_start(step):
        for peer in peers:
            x_copy(step, me, peer).start()
        own_copy(step).start()

    def x_wait(step):
        for peer in peers:
            x_copy(step, peer, peer).wait_recv()
        own_copy(step).wait()

    def z_copies(slot, peer):
        refs = ((tok_ref, ztok), (cot_ref, zcot), (meta_ref, zmeta))
        return [
            pltpu.make_async_remote_copy(
                src_ref=source, dst_ref=target.at[slot],
                send_sem=z_send_sem.at[peer, number], recv_sem=z_recv_sem.at[slot, number],
                device_id=(me, peer), device_id_type=MESH,
            )
            for number, (source, target) in enumerate(refs)
        ]

    def z_dispatch(step):
        source = order[step]
        for copy in z_copies(source, source):
            copy.wait_recv()
        dispatch(step, ztok[source], zcot[source], zmeta[source])
        x_start(step)

    def load_rows(step):
        both = recv[step].reshape(cells, width).astype(jnp.float32)
        rows = [both[j * pair : j * pair + capacity] for j in range(n)]
        grads = [both[j * pair + capacity : (j + 1) * pair] for j in range(n)]
        return (
            jnp.concatenate(rows, axis=0).astype(jnp.bfloat16),
            jnp.concatenate(grads, axis=0).astype(jnp.bfloat16),
        )

    def hidden_values(rows, grads, gate_mat, up_mat, down_mat):
        gate_value = dot(rows, gate_mat)
        up_value = dot(rows, up_mat)
        act_grad = dot(grads, down_mat, 1, 1)
        sig = jax.nn.sigmoid(gate_value)
        silu = gate_value * sig
        activation = (silu * up_value).astype(jnp.bfloat16)
        up_grad = (act_grad * silu).astype(jnp.bfloat16)
        gate_grad = (act_grad * up_value * sig * (1.0 + gate_value * (1.0 - sig))).astype(
            jnp.bfloat16
        )
        return activation, gate_grad, up_grad

    def own_rows():
        rows, grads = load_rows(0)
        out_acc[...] = jnp.zeros_like(out_acc)
        rig_acc[...] = jnp.zeros_like(rig_acc)

        @pl.loop(0, hidden // tile)
        def _(index):
            at = pl.ds(pl.multiple_of(index * tile, tile), tile)
            gate_mat, up_mat, down_mat = wg_ref[:, at], wu_ref[:, at], wd_ref[at, :]
            activation, gate_grad, up_grad = hidden_values(rows, grads, gate_mat, up_mat, down_mat)
            out_acc[...] += dot(activation, down_mat)
            rig_acc[...] += dot(gate_grad, gate_mat, 1, 1) + dot(up_grad, up_mat, 1, 1)

        for j in range(n):
            at = slice(j * capacity, (j + 1) * capacity)
            block = jnp.concatenate([out_acc[at, :], rig_acc[at, :]], axis=0)
            back_send[j] = block.astype(jnp.bfloat16)

    def b_copy(slot, peer):
        return pltpu.make_async_remote_copy(
            src_ref=back_send.at[peer], dst_ref=back_recv.at[slot],
            send_sem=b_send_sem.at[peer], recv_sem=b_recv_sem.at[slot],
            device_id=(peer, group), device_id_type=MESH,
        )

    own_back = pltpu.make_async_copy(back_send.at[me], back_recv.at[me], own_sem.at[4])

    def weight_grads(step):
        rows, grads = load_rows(step)
        half = wgu_s_ref.shape[1] // 2
        activation, gate_grad, up_grad = hidden_values(
            rows, grads, wgu_s_ref[:, :half], wgu_s_ref[:, half:], wd_s_ref[...]
        )
        both = dot(rows, jnp.concatenate([gate_grad, up_grad], axis=1), 0, 0)
        down = dot(activation, grads, 0, 0)[:share]
        gate, up = both[:, :share], both[:, half : half + share]
        for ref, value in ((gate_ref, gate), (up_ref, up), (down_ref, down)):
            if step == 0:
                ref[...] = value
            elif step < 3:
                ref[...] += value
            else:
                ref[...] = (ref[...] + value) * 0.25

    def combine():
        back = back_recv[...].reshape(cells, width)
        cell = lax.broadcasted_iota(jnp.int32, (tok_ref.shape[0], cells), 1)
        cot = cot_ref[...].astype(jnp.float32)
        total = None
        columns = []
        mask = None
        for k in range(2):
            at = index_ref[:, k : k + 1]
            picked = dot(jnp.where(cell == at, 1.0, 0.0).astype(jnp.bfloat16), back)
            term = weight_ref[:, k : k + 1] * picked
            total = term if total is None else total + term
            columns.append(jnp.sum(cot * picked, axis=1, keepdims=True))
            hit = jnp.where(cell - capacity == at, 1.0, 0.0)
            mask = hit if mask is None else mask + hit
        out_ref[...] = total.astype(jnp.bfloat16)
        route_ref[...] = jnp.concatenate(columns, axis=1)
        input_ref[...] = dot(mask.astype(jnp.bfloat16), back).astype(jnp.bfloat16)

    barrier = pltpu.get_barrier_semaphore()
    for peer in peers:
        pl.semaphore_signal(barrier, inc=1, device_id=(peer, group), device_id_type=MESH)
    for peer in order[1:]:
        pl.semaphore_signal(barrier, inc=1, device_id=(me, peer), device_id_type=MESH)
    dispatch(0, tok_ref[...], cot_ref[...], meta_ref[...])
    pl.semaphore_wait(barrier, n - 1 + 3)

    x_start(0)
    for peer in order[1:]:
        for copy in z_copies(group, peer):
            copy.start()
    z_dispatch(1)
    x_wait(0)
    own_rows()
    for peer in peers:
        b_copy(me, peer).start()
    own_back.start()
    z_dispatch(2)
    weight_grads(0)
    x_wait(1)
    weight_grads(1)
    z_dispatch(3)
    x_wait(2)
    weight_grads(2)
    for peer in peers:
        b_copy(peer, peer).wait_recv()
    own_back.wait()
    combine()
    x_wait(3)
    weight_grads(3)

    for peer in order[1:]:
        for copy in z_copies(group, peer):
            copy.wait_send()
    for peer in peers:
        for step in range(4):
            x_copy(step, me, peer).wait_send()
        b_copy(me, peer).wait_send()


def fused(tokens, expert_ids, slot_index, keep_mask, route_weight, cotangent, w_gate, w_up, w_down):
    n = lax.axis_size("expert") * w_gate.shape[0]
    groups = lax.axis_size("dp")
    local, width = tokens.shape
    hidden = w_gate.shape[2]
    capacity = 5 * local // (2 * n)
    pair = 2 * capacity
    cells = n * pair
    share = hidden // groups
    half = -(-share // 128) * 128
    index = jnp.where(keep_mask == 1, expert_ids * pair + slot_index, -cells)
    meta = jnp.concatenate([index.astype(jnp.float32).T, route_weight.T], axis=0)
    meta = jnp.pad(meta, ((0, 4), (0, 0)))
    start = lax.axis_index("dp") * share
    fill = ((0, 0), (0, half - share))
    gate_s = jnp.pad(lax.dynamic_slice_in_dim(w_gate[0], start, share, 1), fill)
    up_s = jnp.pad(lax.dynamic_slice_in_dim(w_up[0], start, share, 1), fill)
    down_s = jnp.pad(lax.dynamic_slice_in_dim(w_down[0], start, share, 0), fill[::-1])
    vmem = pl.BlockSpec(memory_space=pltpu.VMEM)
    bf16, f32 = jnp.bfloat16, jnp.float32
    dma = pltpu.SemaphoreType.DMA
    results = pl.pallas_call(
        functools.partial(kernel, n, capacity, share),
        out_shape=(
            jax.ShapeDtypeStruct((local, width), bf16),
            jax.ShapeDtypeStruct((local, 2), f32),
            jax.ShapeDtypeStruct((local, width), bf16),
            jax.ShapeDtypeStruct((width, share), f32),
            jax.ShapeDtypeStruct((width, share), f32),
            jax.ShapeDtypeStruct((share, width), f32),
        ),
        in_specs=[vmem] * 10,
        out_specs=(vmem,) * 6,
        scratch_shapes=[
            pltpu.VMEM((groups, local, width), bf16),
            pltpu.VMEM((groups, local, width), bf16),
            pltpu.VMEM((groups, 8, local), f32),
            pltpu.VMEM((groups, n, pair, width), bf16),
            pltpu.VMEM((groups, n, pair, width), bf16),
            pltpu.VMEM((n, pair, width), bf16),
            pltpu.VMEM((n, pair, width), bf16),
            pltpu.VMEM((n * capacity, width), f32),
            pltpu.VMEM((n * capacity, width), f32),
            dma((groups, 3)),
            dma((groups, 3)),
            dma((groups, n)),
            dma((groups, n)),
            dma((n,)),
            dma((n,)),
            dma((5,)),
        ],
        compiler_params=pltpu.CompilerParams(
            collective_id=0, has_side_effects=True, vmem_limit_bytes=58 * 2**20
        ),
        cost_estimate=pl.CostEstimate(
            flops=8 * 10**9, bytes_accessed=12 * 2**20, transcendentals=5 * 10**5
        ),
    )(
        tokens, cotangent, meta, index, route_weight, w_gate[0], w_up[0], w_down[0],
        jnp.concatenate([gate_s, up_s], axis=1), down_s,
    )
    return results[:3] + tuple(value[None] for value in results[3:])


def local_program(*args):
    local, hidden = args[0].shape[0], args[6].shape[2]
    n, groups = lax.axis_size("expert") * args[6].shape[0], lax.axis_size("dp")
    capacity = 5 * local // (2 * n)
    fits = groups == 4 and args[6].shape[0] == 1 and capacity % 8 == 0
    if fits and hidden % 256 == 0 and local % 128 == 0:
        return fused(*args)
    return body(*args)


def solution(mesh):
    return jax.shard_map(
        local_program,
        mesh=mesh,
        in_specs=(
            P(("expert", "dp"), None),
            P(("expert", "dp"), None),
            P(("expert", "dp"), None),
            P(("expert", "dp"), None),
            P(("expert", "dp"), None),
            P(("expert", "dp"), None),
            P("expert", None, None),
            P("expert", None, None),
            P("expert", None, None),
        ),
        out_specs=(
            P(("expert", "dp"), None),
            P(("expert", "dp"), None),
            P(("expert", "dp"), None),
            P("expert", None, "dp"),
            P("expert", None, "dp"),
            P("expert", "dp", None),
        ),
        check_vma=False,
    )
```

```python
import functools

import jax
import jax.numpy as jnp
from jax import lax
from jax.experimental import pallas as pl
from jax.experimental.pallas import tpu as pltpu
from jax.sharding import PartitionSpec as P

MESH = pl.DeviceIdType.MESH


def expert_forward(rows_in, gate_mat, up_mat, down_mat):
    gate_value = jnp.dot(rows_in, gate_mat, preferred_element_type=jnp.float32)
    up_value = jnp.dot(rows_in, up_mat, preferred_element_type=jnp.float32)
    sigmoid_gate = jax.nn.sigmoid(gate_value)
    activation = (gate_value * sigmoid_gate * up_value).astype(jnp.bfloat16)
    expert_out = jnp.dot(activation, down_mat, preferred_element_type=jnp.float32).astype(
        jnp.bfloat16
    )
    return (gate_value, up_value, sigmoid_gate, activation, expert_out)


def value_grads(rows_grad, down_mat, gate_value, up_value, sigmoid_gate):
    act_grad = lax.dot_general(
        rows_grad, down_mat, (((1,), (1,)), ((), ())), preferred_element_type=jnp.float32
    )
    up_value_grad = (act_grad * gate_value * sigmoid_gate).astype(jnp.bfloat16)
    gate_value_grad = (
        act_grad * up_value * sigmoid_gate * (1.0 + gate_value * (1.0 - sigmoid_gate))
    ).astype(jnp.bfloat16)
    return (gate_value_grad, up_value_grad)


def column_product(left, right):
    return lax.dot_general(
        left, right, (((0,), (0,)), ((), ())), preferred_element_type=jnp.float32
    )


def body(tokens, expert_ids, slot_index, keep_mask, route_weight, cotangent, w_gate, w_up, w_down):
    groups = lax.axis_size("expert")
    data_groups = lax.axis_size("dp")
    local_tokens = tokens.shape[0]
    width = tokens.shape[1]
    experts_all = groups * w_gate.shape[0]
    capacity = 5 * local_tokens // (2 * experts_all)
    gate_mat = w_gate[0]
    up_mat = w_up[0]
    down_mat = w_down[0]
    flat_index = expert_ids * capacity + slot_index
    cells = jnp.arange(experts_all * capacity, dtype=jnp.int32)
    matrix = ((flat_index[..., None] == cells) & (keep_mask[..., None] == 1)).astype(jnp.bfloat16)
    send_in = jnp.einsum("tkc,td->cd", matrix, tokens, preferred_element_type=jnp.float32)
    send_in = send_in.astype(jnp.bfloat16).reshape(experts_all, capacity, width)
    scaled = (route_weight[..., None] * cotangent[:, None, :].astype(jnp.float32)).astype(
        jnp.bfloat16
    )
    send_grad = jnp.einsum("tkc,tkd->cd", matrix, scaled, preferred_element_type=jnp.float32)
    send_grad = send_grad.astype(jnp.bfloat16).reshape(experts_all, capacity, width)
    rows_in = lax.all_to_all(send_in, "expert", split_axis=0, concat_axis=0, tiled=True)
    rows_in = rows_in.reshape(-1, width)
    gate_value, up_value, sigmoid_gate, activation, expert_out = expert_forward(
        rows_in, gate_mat, up_mat, down_mat
    )
    out_blocks = expert_out.reshape(groups, capacity, width)
    back_out = lax.all_to_all(out_blocks, "expert", split_axis=0, concat_axis=0, tiled=True)
    rows_grad = lax.all_to_all(
        send_grad, "expert", split_axis=0, concat_axis=0, tiled=True
    ).reshape(-1, width)
    part_down = column_product(activation, rows_grad)
    gate_value_grad, up_value_grad = value_grads(
        rows_grad, down_mat, gate_value, up_value, sigmoid_gate
    )
    part_gate = column_product(rows_in, gate_value_grad)
    part_up = column_product(rows_in, up_value_grad)
    gate_sum, up_sum, down_sum = (
        lax.psum_scatter(
            part_gate.astype(jnp.bfloat16), "dp", scatter_dimension=1, tiled=True
        ).astype(jnp.float32),
        lax.psum_scatter(
            part_up.astype(jnp.bfloat16), "dp", scatter_dimension=1, tiled=True
        ).astype(jnp.float32),
        lax.psum_scatter(
            part_down.astype(jnp.bfloat16), "dp", scatter_dimension=0, tiled=True
        ).astype(jnp.float32),
    )
    row_input_grad = lax.dot_general(
        gate_value_grad, gate_mat, (((1,), (1,)), ((), ())), preferred_element_type=jnp.float32
    ) + lax.dot_general(
        up_value_grad, up_mat, (((1,), (1,)), ((), ())), preferred_element_type=jnp.float32
    )
    grad_blocks = row_input_grad.astype(jnp.bfloat16).reshape(groups, capacity, width)
    back_grad = lax.all_to_all(grad_blocks, "expert", split_axis=0, concat_axis=0, tiled=True)
    back_out = back_out.reshape(-1, width)
    back_grad = back_grad.reshape(-1, width)
    picked = jnp.einsum("tkc,cd->tkd", matrix, back_out, preferred_element_type=jnp.float32)
    layer_output = jnp.sum(route_weight[..., None] * picked, axis=1).astype(jnp.bfloat16)
    route_grad = jnp.einsum(
        "td,tkd->tk", cotangent, picked.astype(jnp.bfloat16), preferred_element_type=jnp.float32
    )
    input_grad = jnp.einsum(
        "tkc,cd->td", matrix, back_grad, preferred_element_type=jnp.float32
    ).astype(jnp.bfloat16)
    scale = 1.0 / data_groups
    return (
        layer_output,
        route_grad,
        input_grad,
        (gate_sum * scale)[None],
        (up_sum * scale)[None],
        (down_sum * scale)[None],
    )


def dot(left, right, left_dim=1, right_dim=0):
    return lax.dot_general(
        left, right, (((left_dim,), (right_dim,)), ((), ())), preferred_element_type=jnp.float32
    )


def group_order(index):
    half = index // 2
    side = (1 - half) * index + half * (3 - index)
    order = []
    for step, swapped in enumerate((1, 0, 2, 3)):
        place = (1 - side) * step + side * swapped
        order.append((1 - half) * place + half * (3 - place))
    return order


def kernel(
    n, capacity, share, window,
    tok_ref, cot_ref, ids_ref, slot_ref, keep_ref, weight_ref, wg_ref, wu_ref, wd_ref,
    out_ref, route_ref, input_ref, gate_ref, up_ref, down_ref,
    meta_ref, ztok, zcot, zmeta, send, recv, back_send, back_recv, out_acc, rig_acc, grad_acc,
    z_send_sem, z_recv_sem, x_send_sem, x_recv_sem, b_send_sem, b_recv_sem, own_sem,
):
    me = lax.axis_index("expert")
    group = lax.axis_index("dp")
    order = group_order(group)
    width = tok_ref.shape[1]
    pair = 2 * capacity
    cells = n * pair
    hidden = wg_ref.shape[1]
    tile = 256
    peers = [lax.rem(me + step, n) for step in range(1, n)]
    partner = order[1]
    base = pl.multiple_of(share * group // 128 * 128, 128)
    rest = pl.multiple_of(share * group % 128, 8)

    def dispatch(step, tok, cot, meta):
        first, second = meta[0:1, :], meta[1:2, :]
        w_first, w_second = meta[2:3, :], meta[3:4, :]
        cell = lax.broadcasted_iota(jnp.int32, (cells, tok.shape[0]), 0).astype(jnp.float32)
        to_tok = jnp.where((cell == first) | (cell == second), 1.0, 0.0)
        low = cell - capacity
        hit_first, hit_second = low == first, low == second
        to_cot = jnp.where(hit_first | hit_second, 1.0, 0.0)
        weight = jnp.where(hit_first, w_first, 0.0) + jnp.where(hit_second, w_second, 0.0)
        weight = jnp.sum(weight + to_tok, axis=1, keepdims=True)
        picked = dot(to_tok.astype(jnp.bfloat16), tok) + dot(to_cot.astype(jnp.bfloat16), cot)
        send[step] = (picked * weight).astype(jnp.bfloat16).reshape(n, pair, width)

    def x_copy(step, slot, peer):
        return pltpu.make_async_remote_copy(
            src_ref=send.at[step, peer], dst_ref=recv.at[step, slot],
            send_sem=x_send_sem.at[step, peer], recv_sem=x_recv_sem.at[step, slot],
            device_id=(peer, group), device_id_type=MESH,
        )

    def own_copy(step):
        return pltpu.make_async_copy(send.at[step, me], recv.at[step, me], own_sem.at[step])

    def x_start(step):
        for peer in peers:
            x_copy(step, me, peer).start()
        own_copy(step).start()

    def relay_copy(slot):
        return pltpu.make_async_remote_copy(
            src_ref=recv.at[0, slot], dst_ref=recv.at[1, slot],
            send_sem=x_send_sem.at[1, slot], recv_sem=x_recv_sem.at[1, slot],
            device_id=(me, partner), device_id_type=MESH,
        )

    def x_wait(step):
        for peer in peers:
            x_copy(step, peer, peer).wait_recv()
        own_copy(step).wait()

    def z_copies(slot, peer):
        refs = ((tok_ref, ztok), (cot_ref, zcot), (meta_ref, zmeta))
        return [
            pltpu.make_async_remote_copy(
                src_ref=source, dst_ref=target.at[slot],
                send_sem=z_send_sem.at[peer, number], recv_sem=z_recv_sem.at[slot, number],
                device_id=(me, peer), device_id_type=MESH,
            )
            for number, (source, target) in enumerate(refs)
        ]

    def z_dispatch(step):
        source = order[step]
        for copy in z_copies(source, source):
            copy.wait_recv()
        dispatch(step, ztok[source], zcot[source], zmeta[source])
        x_start(step)

    def load_rows(step):
        both = recv[step].reshape(cells, width).astype(jnp.float32)
        rows = [both[j * pair : j * pair + capacity] for j in range(n)]
        grads = [both[j * pair + capacity : (j + 1) * pair] for j in range(n)]
        return (
            jnp.concatenate(rows, axis=0).astype(jnp.bfloat16),
            jnp.concatenate(grads, axis=0).astype(jnp.bfloat16),
        )

    def hidden_values(rows, grads, gate_mat, up_mat, down_mat):
        gate_value = dot(rows, gate_mat)
        up_value = dot(rows, up_mat)
        act_grad = dot(grads, down_mat, 1, 1)
        sig = jax.nn.sigmoid(gate_value)
        silu = gate_value * sig
        activation = (silu * up_value).astype(jnp.bfloat16)
        up_grad = (act_grad * silu).astype(jnp.bfloat16)
        gate_grad = (act_grad * up_value * sig * (1.0 + gate_value * (1.0 - sig))).astype(
            jnp.bfloat16
        )
        return activation, gate_grad, up_grad

    def own_rows():
        rows, grads = load_rows(0)
        out_acc[...] = jnp.zeros_like(out_acc)
        rig_acc[...] = jnp.zeros_like(rig_acc)

        @pl.loop(0, hidden // tile)
        def _(index):
            at = pl.ds(pl.multiple_of(index * tile, tile), tile)
            gate_mat, up_mat, down_mat = wg_ref[:, at], wu_ref[:, at], wd_ref[at, :]
            activation, gate_grad, up_grad = hidden_values(rows, grads, gate_mat, up_mat, down_mat)
            out_acc[...] += dot(activation, down_mat)
            rig_acc[...] += dot(gate_grad, gate_mat, 1, 1) + dot(up_grad, up_mat, 1, 1)

        for j in range(n):
            at = slice(j * capacity, (j + 1) * capacity)
            block = jnp.concatenate([out_acc[at, :], rig_acc[at, :]], axis=0)
            back_send[j] = block.astype(jnp.bfloat16)

    def b_copy(slot, peer):
        return pltpu.make_async_remote_copy(
            src_ref=back_send.at[peer], dst_ref=back_recv.at[slot],
            send_sem=b_send_sem.at[peer], recv_sem=b_recv_sem.at[slot],
            device_id=(peer, group), device_id_type=MESH,
        )

    own_back = pltpu.make_async_copy(back_send.at[me], back_recv.at[me], own_sem.at[4])

    def weight_grads(step):
        rows, grads = load_rows(step)
        at = pl.ds(base, window)
        activation, gate_grad, up_grad = hidden_values(
            rows, grads, wg_ref[:, at], wu_ref[:, at], wd_ref[at, :]
        )
        parts = ((gate_grad, rows), (up_grad, rows), (activation, grads))
        for number, (left, right) in enumerate(parts):
            value = dot(left, right, 0, 0)
            grad_acc[number] = value if step == 0 else grad_acc[number] + value
        if step == 3:
            for number, ref in enumerate((gate_ref, up_ref, down_ref)):
                ref[...] = grad_acc[number, pl.ds(rest, share), :] * 0.25

    def combine():
        local = tok_ref.shape[0]
        back = back_recv[...].reshape(cells, width)
        cell = lax.broadcasted_iota(jnp.int32, (local, cells), 1).astype(jnp.float32)
        cot = cot_ref[...].astype(jnp.float32)
        turned = jnp.concatenate([meta_ref[...]] * (local // 8), axis=0).T
        lane = lax.broadcasted_iota(jnp.int32, (local, local), 1)
        total = jnp.zeros((local, width), jnp.float32)
        mask = jnp.zeros((local, cells), jnp.float32)
        sums = jnp.zeros((local, local), jnp.float32)
        for k in range(2):
            at = turned[:, k : k + 1]
            picked = dot(jnp.where(cell == at, 1.0, 0.0).astype(jnp.bfloat16), back)
            total += turned[:, k + 2 : k + 3] * picked
            sums = jnp.where(lane == k, jnp.sum(cot * picked, axis=1, keepdims=True), sums)
            mask += jnp.where(cell - capacity == at, 1.0, 0.0)
        out_ref[...] = total.astype(jnp.bfloat16)
        route_ref[...] = sums.T[:2]
        input_ref[...] = dot(mask.astype(jnp.bfloat16), back).astype(jnp.bfloat16)

    barrier = pltpu.get_barrier_semaphore()
    for peer in peers:
        pl.semaphore_signal(barrier, inc=1, device_id=(peer, group), device_id_type=MESH)
    for peer in order[1:]:
        pl.semaphore_signal(barrier, inc=1, device_id=(me, peer), device_id_type=MESH)
    place = jnp.where(keep_ref[...] == 1, ids_ref[...] * pair + slot_ref[...], -cells)
    blank = jnp.zeros((4, tok_ref.shape[0]), jnp.float32)
    meta_ref[...] = jnp.concatenate([place.astype(jnp.float32), weight_ref[...], blank], axis=0)
    dispatch(0, tok_ref[...], cot_ref[...], meta_ref[...])
    pl.semaphore_wait(barrier, n - 1 + 3)

    x_start(0)
    for peer in order[2:]:
        for copy in z_copies(group, peer):
            copy.start()
    for peer in peers:
        x_copy(0, peer, peer).wait_recv()
        relay_copy(peer).start()
    own_copy(0).wait()
    relay_copy(me).start()
    own_rows()
    for peer in peers:
        b_copy(me, peer).start()
    own_back.start()
    z_dispatch(2)
    weight_grads(0)
    z_dispatch(3)
    for slot in range(n):
        relay_copy(slot).wait_recv()
    weight_grads(1)
    for peer in peers:
        b_copy(peer, peer).wait_recv()
    own_back.wait()
    combine()
    x_wait(2)
    weight_grads(2)
    x_wait(3)
    weight_grads(3)

    for peer in order[2:]:
        for copy in z_copies(group, peer):
            copy.wait_send()
    for slot in range(n):
        relay_copy(slot).wait_send()
    for peer in peers:
        for step in (0, 2, 3):
            x_copy(step, me, peer).wait_send()
        b_copy(me, peer).wait_send()


def fused(tokens, expert_ids, slot_index, keep_mask, route_weight, cotangent, w_gate, w_up, w_down):
    n = lax.axis_size("expert") * w_gate.shape[0]
    groups = lax.axis_size("dp")
    local, width = tokens.shape
    hidden = w_gate.shape[2]
    capacity = 5 * local // (2 * n)
    pair = 2 * capacity
    share = hidden // groups
    window = 128 * max(-(-(share * g % 128 + share) // 128) for g in range(groups))
    vmem = pl.BlockSpec(memory_space=pltpu.VMEM)
    bf16, f32 = jnp.bfloat16, jnp.float32
    dma = pltpu.SemaphoreType.DMA
    results = pl.pallas_call(
        functools.partial(kernel, n, capacity, share, window),
        out_shape=(
            jax.ShapeDtypeStruct((local, width), bf16),
            jax.ShapeDtypeStruct((2, local), f32),
            jax.ShapeDtypeStruct((local, width), bf16),
            jax.ShapeDtypeStruct((share, width), f32),
            jax.ShapeDtypeStruct((share, width), f32),
            jax.ShapeDtypeStruct((share, width), f32),
        ),
        in_specs=[vmem] * 9,
        out_specs=(vmem,) * 6,
        scratch_shapes=[
            pltpu.VMEM((8, local), f32),
            pltpu.VMEM((groups, local, width), bf16),
            pltpu.VMEM((groups, local, width), bf16),
            pltpu.VMEM((groups, 8, local), f32),
            pltpu.VMEM((groups, n, pair, width), bf16),
            pltpu.VMEM((groups, n, pair, width), bf16),
            pltpu.VMEM((n, pair, width), bf16),
            pltpu.VMEM((n, pair, width), bf16),
            pltpu.VMEM((n * capacity, width), f32),
            pltpu.VMEM((n * capacity, width), f32),
            pltpu.VMEM((3, window, width), f32),
            dma((groups, 3)),
            dma((groups, 3)),
            dma((groups, n)),
            dma((groups, n)),
            dma((n,)),
            dma((n,)),
            dma((5,)),
        ],
        compiler_params=pltpu.CompilerParams(
            collective_id=0, has_side_effects=True, vmem_limit_bytes=58 * 2**20
        ),
        cost_estimate=pl.CostEstimate(
            flops=8 * 10**9, bytes_accessed=12 * 2**20, transcendentals=5 * 10**5
        ),
    )(
        tokens, cotangent, expert_ids.T, slot_index.T, keep_mask.T, route_weight.T,
        w_gate[0], w_up[0], w_down[0],
    )
    out, route, inputs, gate, up, down = results
    return out, route.T, inputs, gate.T[None], up.T[None], down[None]


def local_program(*args):
    local, hidden = args[0].shape[0], args[6].shape[2]
    n, groups = lax.axis_size("expert") * args[6].shape[0], lax.axis_size("dp")
    capacity = 5 * local // (2 * n)
    fits = groups == 4 and args[6].shape[0] == 1 and capacity % 8 == 0
    if fits and hidden == 768 and local == 128:
        return fused(*args)
    return body(*args)


def solution(mesh):
    return jax.shard_map(
        local_program,
        mesh=mesh,
        in_specs=(
            P(("expert", "dp"), None),
            P(("expert", "dp"), None),
            P(("expert", "dp"), None),
            P(("expert", "dp"), None),
            P(("expert", "dp"), None),
            P(("expert", "dp"), None),
            P("expert", None, None),
            P("expert", None, None),
            P("expert", None, None),
        ),
        out_specs=(
            P(("expert", "dp"), None),
            P(("expert", "dp"), None),
            P(("expert", "dp"), None),
            P("expert", None, "dp"),
            P("expert", None, "dp"),
            P("expert", "dp", None),
        ),
        check_vma=False,
    )
```

```python
import functools

import jax
import jax.numpy as jnp
from jax import lax
from jax.experimental import pallas as pl
from jax.experimental.pallas import tpu as pltpu
from jax.sharding import PartitionSpec as P

MESH = pl.DeviceIdType.MESH


def expert_forward(rows_in, gate_mat, up_mat, down_mat):
    gate_value = jnp.dot(rows_in, gate_mat, preferred_element_type=jnp.float32)
    up_value = jnp.dot(rows_in, up_mat, preferred_element_type=jnp.float32)
    sigmoid_gate = jax.nn.sigmoid(gate_value)
    activation = (gate_value * sigmoid_gate * up_value).astype(jnp.bfloat16)
    expert_out = jnp.dot(activation, down_mat, preferred_element_type=jnp.float32).astype(
        jnp.bfloat16
    )
    return (gate_value, up_value, sigmoid_gate, activation, expert_out)


def value_grads(rows_grad, down_mat, gate_value, up_value, sigmoid_gate):
    act_grad = lax.dot_general(
        rows_grad, down_mat, (((1,), (1,)), ((), ())), preferred_element_type=jnp.float32
    )
    up_value_grad = (act_grad * gate_value * sigmoid_gate).astype(jnp.bfloat16)
    gate_value_grad = (
        act_grad * up_value * sigmoid_gate * (1.0 + gate_value * (1.0 - sigmoid_gate))
    ).astype(jnp.bfloat16)
    return (gate_value_grad, up_value_grad)


def column_product(left, right):
    return lax.dot_general(
        left, right, (((0,), (0,)), ((), ())), preferred_element_type=jnp.float32
    )


def body(tokens, expert_ids, slot_index, keep_mask, route_weight, cotangent, w_gate, w_up, w_down):
    groups = lax.axis_size("expert")
    data_groups = lax.axis_size("dp")
    local_tokens = tokens.shape[0]
    width = tokens.shape[1]
    experts_all = groups * w_gate.shape[0]
    capacity = 5 * local_tokens // (2 * experts_all)
    gate_mat = w_gate[0]
    up_mat = w_up[0]
    down_mat = w_down[0]
    flat_index = expert_ids * capacity + slot_index
    cells = jnp.arange(experts_all * capacity, dtype=jnp.int32)
    matrix = ((flat_index[..., None] == cells) & (keep_mask[..., None] == 1)).astype(jnp.bfloat16)
    send_in = jnp.einsum("tkc,td->cd", matrix, tokens, preferred_element_type=jnp.float32)
    send_in = send_in.astype(jnp.bfloat16).reshape(experts_all, capacity, width)
    scaled = (route_weight[..., None] * cotangent[:, None, :].astype(jnp.float32)).astype(
        jnp.bfloat16
    )
    send_grad = jnp.einsum("tkc,tkd->cd", matrix, scaled, preferred_element_type=jnp.float32)
    send_grad = send_grad.astype(jnp.bfloat16).reshape(experts_all, capacity, width)
    rows_in = lax.all_to_all(send_in, "expert", split_axis=0, concat_axis=0, tiled=True)
    rows_in = rows_in.reshape(-1, width)
    gate_value, up_value, sigmoid_gate, activation, expert_out = expert_forward(
        rows_in, gate_mat, up_mat, down_mat
    )
    out_blocks = expert_out.reshape(groups, capacity, width)
    back_out = lax.all_to_all(out_blocks, "expert", split_axis=0, concat_axis=0, tiled=True)
    rows_grad = lax.all_to_all(
        send_grad, "expert", split_axis=0, concat_axis=0, tiled=True
    ).reshape(-1, width)
    part_down = column_product(activation, rows_grad)
    gate_value_grad, up_value_grad = value_grads(
        rows_grad, down_mat, gate_value, up_value, sigmoid_gate
    )
    part_gate = column_product(rows_in, gate_value_grad)
    part_up = column_product(rows_in, up_value_grad)
    gate_sum, up_sum, down_sum = (
        lax.psum_scatter(
            part_gate.astype(jnp.bfloat16), "dp", scatter_dimension=1, tiled=True
        ).astype(jnp.float32),
        lax.psum_scatter(
            part_up.astype(jnp.bfloat16), "dp", scatter_dimension=1, tiled=True
        ).astype(jnp.float32),
        lax.psum_scatter(
            part_down.astype(jnp.bfloat16), "dp", scatter_dimension=0, tiled=True
        ).astype(jnp.float32),
    )
    row_input_grad = lax.dot_general(
        gate_value_grad, gate_mat, (((1,), (1,)), ((), ())), preferred_element_type=jnp.float32
    ) + lax.dot_general(
        up_value_grad, up_mat, (((1,), (1,)), ((), ())), preferred_element_type=jnp.float32
    )
    grad_blocks = row_input_grad.astype(jnp.bfloat16).reshape(groups, capacity, width)
    back_grad = lax.all_to_all(grad_blocks, "expert", split_axis=0, concat_axis=0, tiled=True)
    back_out = back_out.reshape(-1, width)
    back_grad = back_grad.reshape(-1, width)
    picked = jnp.einsum("tkc,cd->tkd", matrix, back_out, preferred_element_type=jnp.float32)
    layer_output = jnp.sum(route_weight[..., None] * picked, axis=1).astype(jnp.bfloat16)
    route_grad = jnp.einsum(
        "td,tkd->tk", cotangent, picked.astype(jnp.bfloat16), preferred_element_type=jnp.float32
    )
    input_grad = jnp.einsum(
        "tkc,cd->td", matrix, back_grad, preferred_element_type=jnp.float32
    ).astype(jnp.bfloat16)
    scale = 1.0 / data_groups
    return (
        layer_output,
        route_grad,
        input_grad,
        (gate_sum * scale)[None],
        (up_sum * scale)[None],
        (down_sum * scale)[None],
    )


def dot(left, right, left_dim=1, right_dim=0):
    return lax.dot_general(
        left, right, (((left_dim,), (right_dim,)), ((), ())), preferred_element_type=jnp.float32
    )


def group_order(index):
    half = index // 2
    side = (1 - half) * index + half * (3 - index)
    order = []
    for step, swapped in enumerate((1, 0, 2, 3)):
        place = (1 - side) * step + side * swapped
        order.append((1 - half) * place + half * (3 - place))
    return order


def kernel(
    n, capacity, share, window,
    tok_ref, cot_ref, ids_ref, slot_ref, keep_ref, weight_ref, wg_in, wu_in, wd_in,
    out_ref, route_ref, input_ref, gate_ref, up_ref, down_ref,
    meta_ref, ztok, zcot, zmeta, send, recv, back_send, back_recv, out_acc, rig_acc, grad_acc, wg_ref, wu_ref, wd_ref,
    z_send_sem, z_recv_sem, x_send_sem, x_recv_sem, b_send_sem, b_recv_sem, own_sem, weight_sem,
):
    me = lax.axis_index("expert")
    group = lax.axis_index("dp")
    order = group_order(group)
    width = tok_ref.shape[1]
    pair = 2 * capacity
    cells = n * pair
    hidden = wg_ref.shape[1]
    tile = 256
    peers = [lax.rem(me + step, n) for step in range(1, n)]
    partner = order[1]
    base = pl.multiple_of(share * group // 128 * 128, 128)
    rest = pl.multiple_of(share * group % 128, 8)

    def dispatch(step, tok, cot, meta):
        first, second = meta[0:1, :], meta[1:2, :]
        w_first, w_second = meta[2:3, :], meta[3:4, :]
        cell = lax.broadcasted_iota(jnp.int32, (cells, tok.shape[0]), 0).astype(jnp.float32)
        to_tok = jnp.where((cell == first) | (cell == second), 1.0, 0.0)
        low = cell - capacity
        hit_first, hit_second = low == first, low == second
        to_cot = jnp.where(hit_first | hit_second, 1.0, 0.0)
        weight = jnp.where(hit_first, w_first, 0.0) + jnp.where(hit_second, w_second, 0.0)
        weight = jnp.sum(weight + to_tok, axis=1, keepdims=True)
        picked = dot(to_tok.astype(jnp.bfloat16), tok) + dot(to_cot.astype(jnp.bfloat16), cot)
        send[step] = (picked * weight).astype(jnp.bfloat16).reshape(n, pair, width)

    def x_copy(step, slot, peer):
        return pltpu.make_async_remote_copy(
            src_ref=send.at[step, peer], dst_ref=recv.at[step, slot],
            send_sem=x_send_sem.at[step, peer], recv_sem=x_recv_sem.at[step, slot],
            device_id=(peer, group), device_id_type=MESH,
        )

    def own_copy(step):
        return pltpu.make_async_copy(send.at[step, me], recv.at[step, me], own_sem.at[step])

    def x_start(step):
        for peer in peers:
            x_copy(step, me, peer).start()
        own_copy(step).start()

    def relay_copy(slot):
        return pltpu.make_async_remote_copy(
            src_ref=recv.at[0, slot], dst_ref=recv.at[1, slot],
            send_sem=x_send_sem.at[1, slot], recv_sem=x_recv_sem.at[1, slot],
            device_id=(me, partner), device_id_type=MESH,
        )

    def x_wait(step):
        for peer in peers:
            x_copy(step, peer, peer).wait_recv()
        own_copy(step).wait()

    def z_copies(slot, peer, held=False):
        refs = ((tok_ref, ztok), (cot_ref, zcot), (meta_ref, zmeta))
        if held:
            refs = tuple((target.at[slot], target) for _, target in refs)
        return [
            pltpu.make_async_remote_copy(
                src_ref=source, dst_ref=target.at[slot],
                send_sem=z_send_sem.at[slot, number], recv_sem=z_recv_sem.at[slot, number],
                device_id=(me, peer), device_id_type=MESH,
            )
            for number, (source, target) in enumerate(refs)
        ]

    inner = (group == 1) | (group == 2)

    def z_wait(step):
        for copy in z_copies(order[step], order[step]):
            copy.wait_recv()

    def z_forward(step):
        @pl.when(inner)
        def _():
            z_wait(step)
            for copy in z_copies(order[step], partner, held=True):
                copy.start()

    def z_dispatch(step):
        source = order[step]

        @pl.when(jnp.logical_not(inner))
        def _():
            z_wait(step)

        dispatch(step, ztok[source], zcot[source], zmeta[source])
        x_start(step)

    def load_rows(step):
        both = recv[step].reshape(cells, width).astype(jnp.float32)
        rows = [both[j * pair : j * pair + capacity] for j in range(n)]
        grads = [both[j * pair + capacity : (j + 1) * pair] for j in range(n)]
        return (
            jnp.concatenate(rows, axis=0).astype(jnp.bfloat16),
            jnp.concatenate(grads, axis=0).astype(jnp.bfloat16),
        )

    def hidden_values(rows, grads, gate_mat, up_mat, down_mat):
        gate_value = dot(rows, gate_mat)
        up_value = dot(rows, up_mat)
        act_grad = dot(grads, down_mat, 1, 1)
        sig = jax.nn.sigmoid(gate_value)
        silu = gate_value * sig
        activation = (silu * up_value).astype(jnp.bfloat16)
        up_grad = (act_grad * silu).astype(jnp.bfloat16)
        gate_grad = (act_grad * up_value * sig * (1.0 + gate_value * (1.0 - sig))).astype(
            jnp.bfloat16
        )
        return activation, gate_grad, up_grad

    def own_rows():
        rows, grads = load_rows(0)
        out_acc[...] = jnp.zeros_like(out_acc)
        rig_acc[...] = jnp.zeros_like(rig_acc)

        @pl.loop(0, hidden // tile)
        def _(index):
            at = pl.ds(pl.multiple_of(index * tile, tile), tile)
            gate_mat, up_mat, down_mat = wg_ref[:, at], wu_ref[:, at], wd_ref[at, :]
            activation, gate_grad, up_grad = hidden_values(rows, grads, gate_mat, up_mat, down_mat)
            out_acc[...] += dot(activation, down_mat)
            rig_acc[...] += dot(gate_grad, gate_mat, 1, 1) + dot(up_grad, up_mat, 1, 1)

        for j in range(n):
            at = slice(j * capacity, (j + 1) * capacity)
            block = jnp.concatenate([out_acc[at, :], rig_acc[at, :]], axis=0)
            back_send[j] = block.astype(jnp.bfloat16)

    def b_copy(slot, peer):
        return pltpu.make_async_remote_copy(
            src_ref=back_send.at[peer], dst_ref=back_recv.at[slot],
            send_sem=b_send_sem.at[peer], recv_sem=b_recv_sem.at[slot],
            device_id=(peer, group), device_id_type=MESH,
        )

    own_back = pltpu.make_async_copy(back_send.at[me], back_recv.at[me], own_sem.at[4])

    def weight_grads(step):
        rows, grads = load_rows(step)
        at = pl.ds(base, window)
        activation, gate_grad, up_grad = hidden_values(
            rows, grads, wg_ref[:, at], wu_ref[:, at], wd_ref[at, :]
        )
        parts = ((gate_grad, rows), (up_grad, rows), (activation, grads))
        for number, (left, right) in enumerate(parts):
            value = dot(left, right, 0, 0)
            grad_acc[number] = value if step == 0 else grad_acc[number] + value
        if step == 3:
            for number, ref in enumerate((gate_ref, up_ref, down_ref)):
                ref[...] = grad_acc[number, pl.ds(rest, share), :] * 0.25

    def combine():
        local = tok_ref.shape[0]
        back = back_recv[...].reshape(cells, width)
        cell = lax.broadcasted_iota(jnp.int32, (local, cells), 1).astype(jnp.float32)
        cot = cot_ref[...].astype(jnp.float32)
        turned = jnp.concatenate([meta_ref[...]] * (local // 8), axis=0).T
        lane = lax.broadcasted_iota(jnp.int32, (local, local), 1)
        total = jnp.zeros((local, width), jnp.float32)
        mask = jnp.zeros((local, cells), jnp.float32)
        sums = jnp.zeros((local, local), jnp.float32)
        for k in range(2):
            at = turned[:, k : k + 1]
            picked = dot(jnp.where(cell == at, 1.0, 0.0).astype(jnp.bfloat16), back)
            total += turned[:, k + 2 : k + 3] * picked
            sums = jnp.where(lane == k, jnp.sum(cot * picked, axis=1, keepdims=True), sums)
            mask += jnp.where(cell - capacity == at, 1.0, 0.0)
        out_ref[...] = total.astype(jnp.bfloat16)
        route_ref[...] = sums.T[:2]
        input_ref[...] = dot(mask.astype(jnp.bfloat16), back).astype(jnp.bfloat16)

    weights = ((wg_in, wg_ref), (wu_in, wu_ref), (wd_in, wd_ref))
    weight_copies = [
        pltpu.make_async_copy(source, target, weight_sem.at[number])
        for number, (source, target) in enumerate(weights)
    ]
    for copy in weight_copies:
        copy.start()
    barrier = pltpu.get_barrier_semaphore()
    for peer in peers:
        pl.semaphore_signal(barrier, inc=1, device_id=(peer, group), device_id_type=MESH)
    for peer in order[1:]:
        pl.semaphore_signal(barrier, inc=1, device_id=(me, peer), device_id_type=MESH)
    place = jnp.where(keep_ref[...] == 1, ids_ref[...] * pair + slot_ref[...], -cells)
    blank = jnp.zeros((4, tok_ref.shape[0]), jnp.float32)
    meta_ref[...] = jnp.concatenate([place.astype(jnp.float32), weight_ref[...], blank], axis=0)
    dispatch(0, tok_ref[...], cot_ref[...], meta_ref[...])
    pl.semaphore_wait(barrier, n - 1 + 3)

    for copy in z_copies(group, order[2]):
        copy.start()
    x_start(0)
    z_forward(2)
    for peer in peers:
        x_copy(0, peer, peer).wait_recv()
        relay_copy(peer).start()
    own_copy(0).wait()
    relay_copy(me).start()
    z_forward(3)
    for copy in weight_copies:
        copy.wait()
    own_rows()
    for peer in peers:
        b_copy(me, peer).start()
    own_back.start()
    z_dispatch(2)
    weight_grads(0)
    z_dispatch(3)
    for slot in range(n):
        relay_copy(slot).wait_recv()
    weight_grads(1)
    for peer in peers:
        b_copy(peer, peer).wait_recv()
    own_back.wait()
    combine()
    x_wait(2)
    weight_grads(2)
    x_wait(3)
    weight_grads(3)

    for copy in z_copies(group, order[2]):
        copy.wait_send()

    @pl.when(inner)
    def _():
        for source in order[2:]:
            for copy in z_copies(source, partner, held=True):
                copy.wait_send()

    for slot in range(n):
        relay_copy(slot).wait_send()
    for peer in peers:
        for step in (0, 2, 3):
            x_copy(step, me, peer).wait_send()
        b_copy(me, peer).wait_send()


def finish(*refs):
    sems = refs[12]
    copies = [pltpu.make_async_copy(refs[i], refs[6 + i], sems.at[i]) for i in range(6)]
    for copy in copies:
        copy.start()
    for copy in copies:
        copy.wait()


def fused(tokens, expert_ids, slot_index, keep_mask, route_weight, cotangent, w_gate, w_up, w_down):
    n = lax.axis_size("expert") * w_gate.shape[0]
    groups = lax.axis_size("dp")
    local, width = tokens.shape
    hidden = w_gate.shape[2]
    capacity = 5 * local // (2 * n)
    pair = 2 * capacity
    share = hidden // groups
    window = 128 * max(-(-(share * g % 128 + share) // 128) for g in range(groups))
    vmem = pl.BlockSpec(memory_space=pltpu.VMEM)
    bf16, f32 = jnp.bfloat16, jnp.float32
    dma = pltpu.SemaphoreType.DMA
    results = pl.pallas_call(
        functools.partial(kernel, n, capacity, share, window),
        out_shape=(
            jax.ShapeDtypeStruct((local, width), bf16),
            jax.ShapeDtypeStruct((2, local), f32),
            jax.ShapeDtypeStruct((local, width), bf16),
            jax.ShapeDtypeStruct((share, width), f32),
            jax.ShapeDtypeStruct((share, width), f32),
            jax.ShapeDtypeStruct((share, width), f32),
        ),
        in_specs=[vmem] * 6 + [pl.BlockSpec(memory_space=pl.ANY)] * 3,
        out_specs=(vmem,) * 6,
        scratch_shapes=[
            pltpu.VMEM((8, local), f32),
            pltpu.VMEM((groups, local, width), bf16),
            pltpu.VMEM((groups, local, width), bf16),
            pltpu.VMEM((groups, 8, local), f32),
            pltpu.VMEM((groups, n, pair, width), bf16),
            pltpu.VMEM((groups, n, pair, width), bf16),
            pltpu.VMEM((n, pair, width), bf16),
            pltpu.VMEM((n, pair, width), bf16),
            pltpu.VMEM((n * capacity, width), f32),
            pltpu.VMEM((n * capacity, width), f32),
            pltpu.VMEM((3, window, width), f32),
            pltpu.VMEM((width, hidden), bf16),
            pltpu.VMEM((width, hidden), bf16),
            pltpu.VMEM((hidden, width), bf16),
            dma((groups, 3)),
            dma((groups, 3)),
            dma((groups, n)),
            dma((groups, n)),
            dma((n,)),
            dma((n,)),
            dma((5,)),
            dma((3,)),
        ],
        compiler_params=pltpu.CompilerParams(
            collective_id=0, has_side_effects=True, vmem_limit_bytes=58 * 2**20
        ),
        cost_estimate=pl.CostEstimate(
            flops=8 * 10**9, bytes_accessed=12 * 2**20, transcendentals=5 * 10**5
        ),
    )(
        tokens, cotangent, expert_ids.T, slot_index.T, keep_mask.T, route_weight.T,
        w_gate[0], w_up[0], w_down[0],
    )
    place = pl.BlockSpec(memory_space=pl.ANY)
    out, route, inputs, gate, up, down = pl.pallas_call(
        finish,
        out_shape=tuple(jax.ShapeDtypeStruct(value.shape, value.dtype) for value in results),
        in_specs=[place] * 6,
        out_specs=(place,) * 6,
        scratch_shapes=[dma((6,))],
    )(*results)
    return out, route.T, inputs, gate.T[None], up.T[None], down[None]


def local_program(*args):
    local, hidden = args[0].shape[0], args[6].shape[2]
    n, groups = lax.axis_size("expert") * args[6].shape[0], lax.axis_size("dp")
    capacity = 5 * local // (2 * n)
    fits = groups == 4 and args[6].shape[0] == 1 and capacity % 8 == 0
    if fits and hidden == 768 and local == 128:
        return fused(*args)
    return body(*args)


def solution(mesh):
    return jax.shard_map(
        local_program,
        mesh=mesh,
        in_specs=(
            P(("expert", "dp"), None),
            P(("expert", "dp"), None),
            P(("expert", "dp"), None),
            P(("expert", "dp"), None),
            P(("expert", "dp"), None),
            P(("expert", "dp"), None),
            P("expert", None, None),
            P("expert", None, None),
            P("expert", None, None),
        ),
        out_specs=(
            P(("expert", "dp"), None),
            P(("expert", "dp"), None),
            P(("expert", "dp"), None),
            P("expert", None, "dp"),
            P("expert", None, "dp"),
            P("expert", "dp", None),
        ),
        check_vma=False,
    )
```

```python
import functools

import jax
import jax.numpy as jnp
from jax import lax
from jax.experimental import pallas as pl
from jax.experimental.pallas import tpu as pltpu
from jax.sharding import PartitionSpec as P

MESH = pl.DeviceIdType.MESH


def expert_forward(rows_in, gate_mat, up_mat, down_mat):
    gate_value = jnp.dot(rows_in, gate_mat, preferred_element_type=jnp.float32)
    up_value = jnp.dot(rows_in, up_mat, preferred_element_type=jnp.float32)
    sigmoid_gate = jax.nn.sigmoid(gate_value)
    activation = (gate_value * sigmoid_gate * up_value).astype(jnp.bfloat16)
    expert_out = jnp.dot(activation, down_mat, preferred_element_type=jnp.float32).astype(
        jnp.bfloat16
    )
    return (gate_value, up_value, sigmoid_gate, activation, expert_out)


def value_grads(rows_grad, down_mat, gate_value, up_value, sigmoid_gate):
    act_grad = lax.dot_general(
        rows_grad, down_mat, (((1,), (1,)), ((), ())), preferred_element_type=jnp.float32
    )
    up_value_grad = (act_grad * gate_value * sigmoid_gate).astype(jnp.bfloat16)
    gate_value_grad = (
        act_grad * up_value * sigmoid_gate * (1.0 + gate_value * (1.0 - sigmoid_gate))
    ).astype(jnp.bfloat16)
    return (gate_value_grad, up_value_grad)


def column_product(left, right):
    return lax.dot_general(
        left, right, (((0,), (0,)), ((), ())), preferred_element_type=jnp.float32
    )


def body(tokens, expert_ids, slot_index, keep_mask, route_weight, cotangent, w_gate, w_up, w_down):
    groups = lax.axis_size("expert")
    data_groups = lax.axis_size("dp")
    local_tokens = tokens.shape[0]
    width = tokens.shape[1]
    experts_all = groups * w_gate.shape[0]
    capacity = 5 * local_tokens // (2 * experts_all)
    gate_mat = w_gate[0]
    up_mat = w_up[0]
    down_mat = w_down[0]
    flat_index = expert_ids * capacity + slot_index
    cells = jnp.arange(experts_all * capacity, dtype=jnp.int32)
    matrix = ((flat_index[..., None] == cells) & (keep_mask[..., None] == 1)).astype(jnp.bfloat16)
    send_in = jnp.einsum("tkc,td->cd", matrix, tokens, preferred_element_type=jnp.float32)
    send_in = send_in.astype(jnp.bfloat16).reshape(experts_all, capacity, width)
    scaled = (route_weight[..., None] * cotangent[:, None, :].astype(jnp.float32)).astype(
        jnp.bfloat16
    )
    send_grad = jnp.einsum("tkc,tkd->cd", matrix, scaled, preferred_element_type=jnp.float32)
    send_grad = send_grad.astype(jnp.bfloat16).reshape(experts_all, capacity, width)
    rows_in = lax.all_to_all(send_in, "expert", split_axis=0, concat_axis=0, tiled=True)
    rows_in = rows_in.reshape(-1, width)
    gate_value, up_value, sigmoid_gate, activation, expert_out = expert_forward(
        rows_in, gate_mat, up_mat, down_mat
    )
    out_blocks = expert_out.reshape(groups, capacity, width)
    back_out = lax.all_to_all(out_blocks, "expert", split_axis=0, concat_axis=0, tiled=True)
    rows_grad = lax.all_to_all(
        send_grad, "expert", split_axis=0, concat_axis=0, tiled=True
    ).reshape(-1, width)
    part_down = column_product(activation, rows_grad)
    gate_value_grad, up_value_grad = value_grads(
        rows_grad, down_mat, gate_value, up_value, sigmoid_gate
    )
    part_gate = column_product(rows_in, gate_value_grad)
    part_up = column_product(rows_in, up_value_grad)
    gate_sum, up_sum, down_sum = (
        lax.psum_scatter(
            part_gate.astype(jnp.bfloat16), "dp", scatter_dimension=1, tiled=True
        ).astype(jnp.float32),
        lax.psum_scatter(
            part_up.astype(jnp.bfloat16), "dp", scatter_dimension=1, tiled=True
        ).astype(jnp.float32),
        lax.psum_scatter(
            part_down.astype(jnp.bfloat16), "dp", scatter_dimension=0, tiled=True
        ).astype(jnp.float32),
    )
    row_input_grad = lax.dot_general(
        gate_value_grad, gate_mat, (((1,), (1,)), ((), ())), preferred_element_type=jnp.float32
    ) + lax.dot_general(
        up_value_grad, up_mat, (((1,), (1,)), ((), ())), preferred_element_type=jnp.float32
    )
    grad_blocks = row_input_grad.astype(jnp.bfloat16).reshape(groups, capacity, width)
    back_grad = lax.all_to_all(grad_blocks, "expert", split_axis=0, concat_axis=0, tiled=True)
    back_out = back_out.reshape(-1, width)
    back_grad = back_grad.reshape(-1, width)
    picked = jnp.einsum("tkc,cd->tkd", matrix, back_out, preferred_element_type=jnp.float32)
    layer_output = jnp.sum(route_weight[..., None] * picked, axis=1).astype(jnp.bfloat16)
    route_grad = jnp.einsum(
        "td,tkd->tk", cotangent, picked.astype(jnp.bfloat16), preferred_element_type=jnp.float32
    )
    input_grad = jnp.einsum(
        "tkc,cd->td", matrix, back_grad, preferred_element_type=jnp.float32
    ).astype(jnp.bfloat16)
    scale = 1.0 / data_groups
    return (
        layer_output,
        route_grad,
        input_grad,
        (gate_sum * scale)[None],
        (up_sum * scale)[None],
        (down_sum * scale)[None],
    )


def dot(left, right, left_dim=1, right_dim=0):
    return lax.dot_general(
        left, right, (((left_dim,), (right_dim,)), ((), ())), preferred_element_type=jnp.float32
    )


def group_order(index):
    half = index // 2
    side = (1 - half) * index + half * (3 - index)
    order = []
    for step, swapped in enumerate((1, 0, 2, 3)):
        place = (1 - side) * step + side * swapped
        order.append((1 - half) * place + half * (3 - place))
    return order


def kernel(
    n, capacity, share, window,
    tok_ref, cot_ref, ids_ref, slot_ref, keep_ref, weight_ref, wg_ref, wu_ref, wd_ref,
    out_ref, route_ref, input_ref, gate_ref, up_ref, down_ref,
    meta_ref, ztok, zcot, zmeta, send, recv, back_send, back_recv, out_acc, rig_acc, grad_acc,
    z_send_sem, z_recv_sem, x_send_sem, x_recv_sem, b_send_sem, b_recv_sem,
):
    me = lax.axis_index("expert")
    group = lax.axis_index("dp")
    order = group_order(group)
    width = tok_ref.shape[1]
    pair = 2 * capacity
    cells = n * pair
    hidden = wg_ref.shape[1]
    tile = 256
    peers = [lax.rem(me + step, n) for step in range(1, n)]
    partner = order[1]
    base = pl.multiple_of(share * group // 128 * 128, 128)
    rest = pl.multiple_of(share * group % 128, 8)

    def dispatch(step, tok, cot, meta):
        first, second = meta[0:1, :], meta[1:2, :]
        w_first, w_second = meta[2:3, :], meta[3:4, :]
        cell = lax.broadcasted_iota(jnp.int32, (cells, tok.shape[0]), 0).astype(jnp.float32)
        to_tok = jnp.where((cell == first) | (cell == second), 1.0, 0.0)
        low = cell - capacity
        hit_first, hit_second = low == first, low == second
        to_cot = jnp.where(hit_first | hit_second, 1.0, 0.0)
        weight = jnp.where(hit_first, w_first, 0.0) + jnp.where(hit_second, w_second, 0.0)
        weight = jnp.sum(weight + to_tok, axis=1, keepdims=True)
        picked = dot(to_tok.astype(jnp.bfloat16), tok) + dot(to_cot.astype(jnp.bfloat16), cot)
        send[step] = (picked * weight).astype(jnp.bfloat16).reshape(n, pair, width)

    def x_copy(step, slot, peer):
        return pltpu.make_async_remote_copy(
            src_ref=send.at[step, peer], dst_ref=recv.at[step, slot],
            send_sem=x_send_sem.at[step, peer], recv_sem=x_recv_sem.at[step, slot],
            device_id=(peer, group), device_id_type=MESH,
        )

    def x_start(step):
        for peer in peers:
            x_copy(step, me, peer).start()
        recv[step, me] = send[step, me]

    def relay_copy(slot):
        return pltpu.make_async_remote_copy(
            src_ref=recv.at[0, slot], dst_ref=recv.at[1, slot],
            send_sem=x_send_sem.at[1, slot], recv_sem=x_recv_sem.at[1, slot],
            device_id=(me, partner), device_id_type=MESH,
        )

    def x_wait(step):
        for peer in peers:
            x_copy(step, peer, peer).wait_recv()

    def z_copies(slot, peer):
        refs = ((tok_ref, ztok), (cot_ref, zcot), (meta_ref, zmeta))
        return [
            pltpu.make_async_remote_copy(
                src_ref=source, dst_ref=target.at[slot],
                send_sem=z_send_sem.at[peer, number], recv_sem=z_recv_sem.at[slot, number],
                device_id=(me, peer), device_id_type=MESH,
            )
            for number, (source, target) in enumerate(refs)
        ]

    def z_dispatch(step):
        source = order[step]
        for copy in z_copies(source, source):
            copy.wait_recv()
        dispatch(step, ztok[source], zcot[source], zmeta[source])
        x_start(step)

    def load_rows(step):
        both = recv[step].reshape(cells, width).astype(jnp.float32)
        rows = [both[j * pair : j * pair + capacity] for j in range(n)]
        grads = [both[j * pair + capacity : (j + 1) * pair] for j in range(n)]
        return (
            jnp.concatenate(rows, axis=0).astype(jnp.bfloat16),
            jnp.concatenate(grads, axis=0).astype(jnp.bfloat16),
        )

    def hidden_values(rows, grads, gate_mat, up_mat, down_mat):
        gate_value = dot(rows, gate_mat)
        up_value = dot(rows, up_mat)
        act_grad = dot(grads, down_mat, 1, 1)
        sig = jax.nn.sigmoid(gate_value)
        silu = gate_value * sig
        activation = (silu * up_value).astype(jnp.bfloat16)
        up_grad = (act_grad * silu).astype(jnp.bfloat16)
        gate_grad = (act_grad * up_value * sig * (1.0 + gate_value * (1.0 - sig))).astype(
            jnp.bfloat16
        )
        return activation, gate_grad, up_grad

    def own_rows():
        rows, grads = load_rows(0)
        out_acc[...] = jnp.zeros_like(out_acc)
        rig_acc[...] = jnp.zeros_like(rig_acc)

        @pl.loop(0, hidden // tile)
        def _(index):
            at = pl.ds(pl.multiple_of(index * tile, tile), tile)
            gate_mat, up_mat, down_mat = wg_ref[:, at], wu_ref[:, at], wd_ref[at, :]
            activation, gate_grad, up_grad = hidden_values(rows, grads, gate_mat, up_mat, down_mat)
            out_acc[...] += dot(activation, down_mat)
            rig_acc[...] += dot(gate_grad, gate_mat, 1, 1) + dot(up_grad, up_mat, 1, 1)

        for j in range(n):
            at = slice(j * capacity, (j + 1) * capacity)
            block = jnp.concatenate([out_acc[at, :], rig_acc[at, :]], axis=0)
            back_send[j] = block.astype(jnp.bfloat16)

    def b_copy(slot, peer):
        return pltpu.make_async_remote_copy(
            src_ref=back_send.at[peer], dst_ref=back_recv.at[slot],
            send_sem=b_send_sem.at[peer], recv_sem=b_recv_sem.at[slot],
            device_id=(peer, group), device_id_type=MESH,
        )

    def weight_grads(step):
        rows, grads = load_rows(step)
        at = pl.ds(base, window)
        activation, gate_grad, up_grad = hidden_values(
            rows, grads, wg_ref[:, at], wu_ref[:, at], wd_ref[at, :]
        )
        parts = ((gate_grad, rows), (up_grad, rows), (activation, grads))
        for number, (left, right) in enumerate(parts):
            value = dot(left, right, 0, 0)
            grad_acc[number] = value if step == 0 else grad_acc[number] + value
        if step == 3:
            for number, ref in enumerate((gate_ref, up_ref, down_ref)):
                ref[...] = grad_acc[number, pl.ds(rest, share), :] * 0.25

    def combine():
        local = tok_ref.shape[0]
        back = back_recv[...].reshape(cells, width)
        cell = lax.broadcasted_iota(jnp.int32, (local, cells), 1).astype(jnp.float32)
        cot = cot_ref[...].astype(jnp.float32)
        turned = jnp.concatenate([meta_ref[...]] * (local // 8), axis=0).T
        lane = lax.broadcasted_iota(jnp.int32, (local, local), 1)
        total = jnp.zeros((local, width), jnp.float32)
        mask = jnp.zeros((local, cells), jnp.float32)
        sums = jnp.zeros((local, local), jnp.float32)
        for k in range(2):
            at = turned[:, k : k + 1]
            picked = dot(jnp.where(cell == at, 1.0, 0.0).astype(jnp.bfloat16), back)
            total += turned[:, k + 2 : k + 3] * picked
            sums = jnp.where(lane == k, jnp.sum(cot * picked, axis=1, keepdims=True), sums)
            mask += jnp.where(cell - capacity == at, 1.0, 0.0)
        out_ref[...] = total.astype(jnp.bfloat16)
        route_ref[...] = sums.T[:2]
        input_ref[...] = dot(mask.astype(jnp.bfloat16), back).astype(jnp.bfloat16)

    barrier = pltpu.get_barrier_semaphore()
    for peer in peers:
        pl.semaphore_signal(barrier, inc=1, device_id=(peer, group), device_id_type=MESH)
    for peer in order[1:]:
        pl.semaphore_signal(barrier, inc=1, device_id=(me, peer), device_id_type=MESH)
    place = jnp.where(keep_ref[...] == 1, ids_ref[...] * pair + slot_ref[...], -cells)
    blank = jnp.zeros((4, tok_ref.shape[0]), jnp.float32)
    meta_ref[...] = jnp.concatenate([place.astype(jnp.float32), weight_ref[...], blank], axis=0)
    dispatch(0, tok_ref[...], cot_ref[...], meta_ref[...])
    pl.semaphore_wait(barrier, n - 1 + 3)

    x_start(0)
    for peer in order[2:]:
        for copy in z_copies(group, peer):
            copy.start()
    for peer in peers:
        x_copy(0, peer, peer).wait_recv()
        relay_copy(peer).start()
    relay_copy(me).start()
    own_rows()
    for peer in peers:
        b_copy(me, peer).start()
    back_recv[me] = back_send[me]
    z_dispatch(2)
    weight_grads(0)
    z_dispatch(3)
    for slot in range(n):
        relay_copy(slot).wait_recv()
    weight_grads(1)
    for peer in peers:
        b_copy(peer, peer).wait_recv()
    combine()
    x_wait(2)
    weight_grads(2)
    x_wait(3)
    weight_grads(3)

    for peer in order[2:]:
        for copy in z_copies(group, peer):
            copy.wait_send()
    for slot in range(n):
        relay_copy(slot).wait_send()
    for peer in peers:
        for step in (0, 2, 3):
            x_copy(step, me, peer).wait_send()
        b_copy(me, peer).wait_send()


def finish(*refs):
    for source, target in zip(refs[:6], refs[6:]):
        target[...] = source[...]


def fused(tokens, expert_ids, slot_index, keep_mask, route_weight, cotangent, w_gate, w_up, w_down):
    n = lax.axis_size("expert") * w_gate.shape[0]
    groups = lax.axis_size("dp")
    local, width = tokens.shape
    hidden = w_gate.shape[2]
    capacity = 5 * local // (2 * n)
    pair = 2 * capacity
    share = hidden // groups
    window = 128 * max(-(-(share * g % 128 + share) // 128) for g in range(groups))
    vmem = pl.BlockSpec(memory_space=pltpu.VMEM)
    bf16, f32 = jnp.bfloat16, jnp.float32
    dma = pltpu.SemaphoreType.DMA
    results = pl.pallas_call(
        functools.partial(kernel, n, capacity, share, window),
        out_shape=(
            jax.ShapeDtypeStruct((local, width), bf16),
            jax.ShapeDtypeStruct((2, local), f32),
            jax.ShapeDtypeStruct((local, width), bf16),
            jax.ShapeDtypeStruct((share, width), f32),
            jax.ShapeDtypeStruct((share, width), f32),
            jax.ShapeDtypeStruct((share, width), f32),
        ),
        in_specs=[vmem] * 9,
        out_specs=(vmem,) * 6,
        scratch_shapes=[
            pltpu.VMEM((8, local), f32),
            pltpu.VMEM((groups, local, width), bf16),
            pltpu.VMEM((groups, local, width), bf16),
            pltpu.VMEM((groups, 8, local), f32),
            pltpu.VMEM((groups, n, pair, width), bf16),
            pltpu.VMEM((groups, n, pair, width), bf16),
            pltpu.VMEM((n, pair, width), bf16),
            pltpu.VMEM((n, pair, width), bf16),
            pltpu.VMEM((n * capacity, width), f32),
            pltpu.VMEM((n * capacity, width), f32),
            pltpu.VMEM((3, window, width), f32),
            dma((groups, 3)),
            dma((groups, 3)),
            dma((groups, n)),
            dma((groups, n)),
            dma((n,)),
            dma((n,)),
        ],
        compiler_params=pltpu.CompilerParams(
            collective_id=0, has_side_effects=True, vmem_limit_bytes=58 * 2**20
        ),
        cost_estimate=pl.CostEstimate(
            flops=8 * 10**9, bytes_accessed=12 * 2**20, transcendentals=5 * 10**5
        ),
    )(
        tokens, cotangent, expert_ids.T, slot_index.T, keep_mask.T, route_weight.T,
        w_gate[0], w_up[0], w_down[0],
    )
    out, route, inputs, gate, up, down = pl.pallas_call(
        finish,
        out_shape=tuple(jax.ShapeDtypeStruct(value.shape, value.dtype) for value in results),
        in_specs=[vmem] * 6,
        out_specs=(vmem,) * 6,
        compiler_params=pltpu.CompilerParams(vmem_limit_bytes=16 * 2**20),
    )(*results)
    return out, route.T, inputs, gate.T[None], up.T[None], down[None]


def local_program(*args):
    local, hidden = args[0].shape[0], args[6].shape[2]
    n, groups = lax.axis_size("expert") * args[6].shape[0], lax.axis_size("dp")
    capacity = 5 * local // (2 * n)
    fits = groups == 4 and args[6].shape[0] == 1 and capacity % 8 == 0
    if fits and hidden == 768 and local == 128:
        return fused(*args)
    return body(*args)


def solution(mesh):
    return jax.shard_map(
        local_program,
        mesh=mesh,
        in_specs=(
            P(("expert", "dp"), None),
            P(("expert", "dp"), None),
            P(("expert", "dp"), None),
            P(("expert", "dp"), None),
            P(("expert", "dp"), None),
            P(("expert", "dp"), None),
            P("expert", None, None),
            P("expert", None, None),
            P("expert", None, None),
        ),
        out_specs=(
            P(("expert", "dp"), None),
            P(("expert", "dp"), None),
            P(("expert", "dp"), None),
            P("expert", None, "dp"),
            P("expert", None, "dp"),
            P("expert", "dp", None),
        ),
        check_vma=False,
    )
```

```python
import functools

import jax
import jax.numpy as jnp
from jax import lax
from jax.experimental import pallas as pl
from jax.experimental.pallas import tpu as pltpu
from jax.sharding import PartitionSpec as P

MESH = pl.DeviceIdType.MESH


def expert_forward(rows_in, gate_mat, up_mat, down_mat):
    gate_value = jnp.dot(rows_in, gate_mat, preferred_element_type=jnp.float32)
    up_value = jnp.dot(rows_in, up_mat, preferred_element_type=jnp.float32)
    sigmoid_gate = jax.nn.sigmoid(gate_value)
    activation = (gate_value * sigmoid_gate * up_value).astype(jnp.bfloat16)
    expert_out = jnp.dot(activation, down_mat, preferred_element_type=jnp.float32).astype(
        jnp.bfloat16
    )
    return (gate_value, up_value, sigmoid_gate, activation, expert_out)


def value_grads(rows_grad, down_mat, gate_value, up_value, sigmoid_gate):
    act_grad = lax.dot_general(
        rows_grad, down_mat, (((1,), (1,)), ((), ())), preferred_element_type=jnp.float32
    )
    up_value_grad = (act_grad * gate_value * sigmoid_gate).astype(jnp.bfloat16)
    gate_value_grad = (
        act_grad * up_value * sigmoid_gate * (1.0 + gate_value * (1.0 - sigmoid_gate))
    ).astype(jnp.bfloat16)
    return (gate_value_grad, up_value_grad)


def column_product(left, right):
    return lax.dot_general(
        left, right, (((0,), (0,)), ((), ())), preferred_element_type=jnp.float32
    )


def body(tokens, expert_ids, slot_index, keep_mask, route_weight, cotangent, w_gate, w_up, w_down):
    groups = lax.axis_size("expert")
    data_groups = lax.axis_size("dp")
    local_tokens = tokens.shape[0]
    width = tokens.shape[1]
    experts_all = groups * w_gate.shape[0]
    capacity = 5 * local_tokens // (2 * experts_all)
    gate_mat = w_gate[0]
    up_mat = w_up[0]
    down_mat = w_down[0]
    flat_index = expert_ids * capacity + slot_index
    cells = jnp.arange(experts_all * capacity, dtype=jnp.int32)
    matrix = ((flat_index[..., None] == cells) & (keep_mask[..., None] == 1)).astype(jnp.bfloat16)
    send_in = jnp.einsum("tkc,td->cd", matrix, tokens, preferred_element_type=jnp.float32)
    send_in = send_in.astype(jnp.bfloat16).reshape(experts_all, capacity, width)
    scaled = (route_weight[..., None] * cotangent[:, None, :].astype(jnp.float32)).astype(
        jnp.bfloat16
    )
    send_grad = jnp.einsum("tkc,tkd->cd", matrix, scaled, preferred_element_type=jnp.float32)
    send_grad = send_grad.astype(jnp.bfloat16).reshape(experts_all, capacity, width)
    rows_in = lax.all_to_all(send_in, "expert", split_axis=0, concat_axis=0, tiled=True)
    rows_in = rows_in.reshape(-1, width)
    gate_value, up_value, sigmoid_gate, activation, expert_out = expert_forward(
        rows_in, gate_mat, up_mat, down_mat
    )
    out_blocks = expert_out.reshape(groups, capacity, width)
    back_out = lax.all_to_all(out_blocks, "expert", split_axis=0, concat_axis=0, tiled=True)
    rows_grad = lax.all_to_all(
        send_grad, "expert", split_axis=0, concat_axis=0, tiled=True
    ).reshape(-1, width)
    part_down = column_product(activation, rows_grad)
    gate_value_grad, up_value_grad = value_grads(
        rows_grad, down_mat, gate_value, up_value, sigmoid_gate
    )
    part_gate = column_product(rows_in, gate_value_grad)
    part_up = column_product(rows_in, up_value_grad)
    gate_sum, up_sum, down_sum = (
        lax.psum_scatter(
            part_gate.astype(jnp.bfloat16), "dp", scatter_dimension=1, tiled=True
        ).astype(jnp.float32),
        lax.psum_scatter(
            part_up.astype(jnp.bfloat16), "dp", scatter_dimension=1, tiled=True
        ).astype(jnp.float32),
        lax.psum_scatter(
            part_down.astype(jnp.bfloat16), "dp", scatter_dimension=0, tiled=True
        ).astype(jnp.float32),
    )
    row_input_grad = lax.dot_general(
        gate_value_grad, gate_mat, (((1,), (1,)), ((), ())), preferred_element_type=jnp.float32
    ) + lax.dot_general(
        up_value_grad, up_mat, (((1,), (1,)), ((), ())), preferred_element_type=jnp.float32
    )
    grad_blocks = row_input_grad.astype(jnp.bfloat16).reshape(groups, capacity, width)
    back_grad = lax.all_to_all(grad_blocks, "expert", split_axis=0, concat_axis=0, tiled=True)
    back_out = back_out.reshape(-1, width)
    back_grad = back_grad.reshape(-1, width)
    picked = jnp.einsum("tkc,cd->tkd", matrix, back_out, preferred_element_type=jnp.float32)
    layer_output = jnp.sum(route_weight[..., None] * picked, axis=1).astype(jnp.bfloat16)
    route_grad = jnp.einsum(
        "td,tkd->tk", cotangent, picked.astype(jnp.bfloat16), preferred_element_type=jnp.float32
    )
    input_grad = jnp.einsum(
        "tkc,cd->td", matrix, back_grad, preferred_element_type=jnp.float32
    ).astype(jnp.bfloat16)
    scale = 1.0 / data_groups
    return (
        layer_output,
        route_grad,
        input_grad,
        (gate_sum * scale)[None],
        (up_sum * scale)[None],
        (down_sum * scale)[None],
    )


def dot(left, right, left_dim=1, right_dim=0):
    return lax.dot_general(
        left, right, (((left_dim,), (right_dim,)), ((), ())), preferred_element_type=jnp.float32
    )


def group_order(index):
    half = index // 2
    side = (1 - half) * index + half * (3 - index)
    order = []
    for step, swapped in enumerate((1, 0, 2, 3)):
        place = (1 - side) * step + side * swapped
        order.append((1 - half) * place + half * (3 - place))
    return order


def kernel(
    n, capacity, share, window,
    tok_ref, cot_ref, ids_ref, slot_ref, keep_ref, weight_ref, wg_ref, wu_ref, wd_ref,
    out_ref, route_ref, input_ref, gate_ref, up_ref, down_ref,
    meta_ref, ztok, zcot, zmeta, send, recv, back_send, back_recv, out_acc, rig_acc, grad_acc,
    z_send_sem, z_recv_sem, x_send_sem, x_recv_sem, b_send_sem, b_recv_sem,
):
    me = lax.axis_index("expert")
    group = lax.axis_index("dp")
    order = group_order(group)
    width = tok_ref.shape[1]
    pair = 2 * capacity
    cells = n * pair
    hidden = wg_ref.shape[1]
    tile = 256
    peers = [lax.rem(me + step, n) for step in range(1, n)]
    partner = order[1]
    base = pl.multiple_of(share * group // 128 * 128, 128)
    rest = pl.multiple_of(share * group % 128, 8)

    def dispatch(step, tok, cot, meta):
        first, second = meta[0:1, :], meta[1:2, :]
        w_first, w_second = meta[2:3, :], meta[3:4, :]
        cell = lax.broadcasted_iota(jnp.int32, (cells, tok.shape[0]), 0).astype(jnp.float32)
        to_tok = jnp.where((cell == first) | (cell == second), 1.0, 0.0)
        low = cell - capacity
        hit_first, hit_second = low == first, low == second
        to_cot = jnp.where(hit_first | hit_second, 1.0, 0.0)
        weight = jnp.where(hit_first, w_first, 0.0) + jnp.where(hit_second, w_second, 0.0)
        weight = jnp.sum(weight + to_tok, axis=1, keepdims=True)
        picked = dot(to_tok.astype(jnp.bfloat16), tok) + dot(to_cot.astype(jnp.bfloat16), cot)
        send[step] = (picked * weight).astype(jnp.bfloat16).reshape(n, pair, width)

    def x_copy(step, slot, peer):
        return pltpu.make_async_remote_copy(
            src_ref=send.at[step, peer], dst_ref=recv.at[step, slot],
            send_sem=x_send_sem.at[step, peer], recv_sem=x_recv_sem.at[step, slot],
            device_id=(peer, group), device_id_type=MESH,
        )

    def x_start(step):
        for peer in peers:
            x_copy(step, me, peer).start()
        recv[step, me] = send[step, me]

    def relay_copy(slot):
        return pltpu.make_async_remote_copy(
            src_ref=recv.at[0, slot], dst_ref=recv.at[1, slot],
            send_sem=x_send_sem.at[1, slot], recv_sem=x_recv_sem.at[1, slot],
            device_id=(me, partner), device_id_type=MESH,
        )

    def x_wait(step):
        for peer in peers:
            x_copy(step, peer, peer).wait_recv()

    def z_copies(slot, peer):
        refs = ((tok_ref, ztok), (cot_ref, zcot), (meta_ref, zmeta))
        return [
            pltpu.make_async_remote_copy(
                src_ref=source, dst_ref=target.at[slot],
                send_sem=z_send_sem.at[peer, number], recv_sem=z_recv_sem.at[slot, number],
                device_id=(me, peer), device_id_type=MESH,
            )
            for number, (source, target) in enumerate(refs)
        ]

    def z_dispatch(step):
        source = order[step]
        for copy in z_copies(source, source):
            copy.wait_recv()
        dispatch(step, ztok[source], zcot[source], zmeta[source])
        x_start(step)

    def load_rows(step):
        both = recv[step].reshape(cells, width).astype(jnp.float32)
        rows = [both[j * pair : j * pair + capacity] for j in range(n)]
        grads = [both[j * pair + capacity : (j + 1) * pair] for j in range(n)]
        return (
            jnp.concatenate(rows, axis=0).astype(jnp.bfloat16),
            jnp.concatenate(grads, axis=0).astype(jnp.bfloat16),
        )

    def hidden_values(rows, grads, gate_mat, up_mat, down_mat):
        gate_value = dot(rows, gate_mat)
        up_value = dot(rows, up_mat)
        act_grad = dot(grads, down_mat, 1, 1)
        sig = jax.nn.sigmoid(gate_value)
        silu = gate_value * sig
        activation = (silu * up_value).astype(jnp.bfloat16)
        up_grad = (act_grad * silu).astype(jnp.bfloat16)
        gate_grad = (act_grad * up_value * sig * (1.0 + gate_value * (1.0 - sig))).astype(
            jnp.bfloat16
        )
        return activation, gate_grad, up_grad

    def own_rows():
        rows, grads = load_rows(0)
        out_acc[...] = jnp.zeros_like(out_acc)
        rig_acc[...] = jnp.zeros_like(rig_acc)

        @pl.loop(0, hidden // tile)
        def _(index):
            at = pl.ds(pl.multiple_of(index * tile, tile), tile)
            gate_mat, up_mat, down_mat = wg_ref[:, at], wu_ref[:, at], wd_ref[at, :]
            activation, gate_grad, up_grad = hidden_values(rows, grads, gate_mat, up_mat, down_mat)
            out_acc[...] += dot(activation, down_mat)
            rig_acc[...] += dot(gate_grad, gate_mat, 1, 1) + dot(up_grad, up_mat, 1, 1)

        for j in range(n):
            at = slice(j * capacity, (j + 1) * capacity)
            block = jnp.concatenate([out_acc[at, :], rig_acc[at, :]], axis=0)
            back_send[j] = block.astype(jnp.bfloat16)

    def b_copy(slot, peer):
        return pltpu.make_async_remote_copy(
            src_ref=back_send.at[peer], dst_ref=back_recv.at[slot],
            send_sem=b_send_sem.at[peer], recv_sem=b_recv_sem.at[slot],
            device_id=(peer, group), device_id_type=MESH,
        )

    def weight_grads(step):
        rows, grads = load_rows(step)
        at = pl.ds(base, window)
        activation, gate_grad, up_grad = hidden_values(
            rows, grads, wg_ref[:, at], wu_ref[:, at], wd_ref[at, :]
        )
        parts = ((gate_grad, rows), (up_grad, rows), (activation, grads))
        for number, (left, right) in enumerate(parts):
            value = dot(left, right, 0, 0)
            grad_acc[number] = value if step == 0 else grad_acc[number] + value
        if step == 3:
            for number, ref in enumerate((gate_ref, up_ref, down_ref)):
                ref[...] = grad_acc[number, pl.ds(rest, share), :] * 0.25

    def combine():
        local = tok_ref.shape[0]
        back = back_recv[...].reshape(cells, width)
        cell = lax.broadcasted_iota(jnp.int32, (local, cells), 1).astype(jnp.float32)
        cot = cot_ref[...].astype(jnp.float32)
        turned = jnp.concatenate([meta_ref[...]] * (local // 8), axis=0).T
        lane = lax.broadcasted_iota(jnp.int32, (local, local), 1)
        total = jnp.zeros((local, width), jnp.float32)
        mask = jnp.zeros((local, cells), jnp.float32)
        sums = jnp.zeros((local, local), jnp.float32)
        for k in range(2):
            at = turned[:, k : k + 1]
            picked = dot(jnp.where(cell == at, 1.0, 0.0).astype(jnp.bfloat16), back)
            total += turned[:, k + 2 : k + 3] * picked
            sums = jnp.where(lane == k, jnp.sum(cot * picked, axis=1, keepdims=True), sums)
            mask += jnp.where(cell - capacity == at, 1.0, 0.0)
        out_ref[...] = total.astype(jnp.bfloat16)
        route_ref[...] = sums.T[:2]
        input_ref[...] = dot(mask.astype(jnp.bfloat16), back).astype(jnp.bfloat16)

    barrier = pltpu.get_barrier_semaphore()
    for peer in peers:
        pl.semaphore_signal(barrier, inc=1, device_id=(peer, group), device_id_type=MESH)
    for peer in order[1:]:
        pl.semaphore_signal(barrier, inc=1, device_id=(me, peer), device_id_type=MESH)
    place = jnp.where(keep_ref[...] == 1, ids_ref[...] * pair + slot_ref[...], -cells)
    blank = jnp.zeros((4, tok_ref.shape[0]), jnp.float32)
    meta_ref[...] = jnp.concatenate([place.astype(jnp.float32), weight_ref[...], blank], axis=0)
    dispatch(0, tok_ref[...], cot_ref[...], meta_ref[...])
    pl.semaphore_wait(barrier, n - 1 + 3)

    x_start(0)
    for peer in order[2:]:
        for copy in z_copies(group, peer):
            copy.start()
    for peer in peers:
        x_copy(0, peer, peer).wait_recv()
        relay_copy(peer).start()
    relay_copy(me).start()
    own_rows()
    for peer in peers:
        b_copy(me, peer).start()
    back_recv[me] = back_send[me]
    z_dispatch(2)
    weight_grads(0)
    z_dispatch(3)
    for slot in range(n):
        relay_copy(slot).wait_recv()
    weight_grads(1)
    for peer in peers:
        b_copy(peer, peer).wait_recv()
    combine()
    x_wait(2)
    weight_grads(2)
    x_wait(3)
    weight_grads(3)

    for peer in order[2:]:
        for copy in z_copies(group, peer):
            copy.wait_send()
    for slot in range(n):
        relay_copy(slot).wait_send()
    for peer in peers:
        for step in (0, 2, 3):
            x_copy(step, me, peer).wait_send()
        b_copy(me, peer).wait_send()


def finish(*refs):
    for source, target in zip(refs[:6], refs[6:]):
        target[...] = source[...]


def fused(tokens, expert_ids, slot_index, keep_mask, route_weight, cotangent, w_gate, w_up, w_down):
    n = lax.axis_size("expert") * w_gate.shape[0]
    groups = lax.axis_size("dp")
    local, width = tokens.shape
    hidden = w_gate.shape[2]
    capacity = 5 * local // (2 * n)
    pair = 2 * capacity
    share = hidden // groups
    window = 128 * max(-(-(share * g % 128 + share) // 128) for g in range(groups))
    vmem = pl.BlockSpec(memory_space=pltpu.VMEM)
    bf16, f32 = jnp.bfloat16, jnp.float32
    dma = pltpu.SemaphoreType.DMA
    results = pl.pallas_call(
        functools.partial(kernel, n, capacity, share, window),
        out_shape=(
            jax.ShapeDtypeStruct((local, width), bf16),
            jax.ShapeDtypeStruct((2, local), f32),
            jax.ShapeDtypeStruct((local, width), bf16),
            jax.ShapeDtypeStruct((share, width), f32),
            jax.ShapeDtypeStruct((share, width), f32),
            jax.ShapeDtypeStruct((share, width), f32),
        ),
        in_specs=[vmem] * 9,
        out_specs=(vmem,) * 6,
        scratch_shapes=[
            pltpu.VMEM((8, local), f32),
            pltpu.VMEM((groups, local, width), bf16),
            pltpu.VMEM((groups, local, width), bf16),
            pltpu.VMEM((groups, 8, local), f32),
            pltpu.VMEM((groups, n, pair, width), bf16),
            pltpu.VMEM((groups, n, pair, width), bf16),
            pltpu.VMEM((n, pair, width), bf16),
            pltpu.VMEM((n, pair, width), bf16),
            pltpu.VMEM((n * capacity, width), f32),
            pltpu.VMEM((n * capacity, width), f32),
            pltpu.VMEM((3, window, width), f32),
            dma((groups, 3)),
            dma((groups, 3)),
            dma((groups, n)),
            dma((groups, n)),
            dma((n,)),
            dma((n,)),
        ],
        compiler_params=pltpu.CompilerParams(
            collective_id=0, has_side_effects=True, vmem_limit_bytes=58 * 2**20
        ),
        cost_estimate=pl.CostEstimate(
            flops=8 * 10**9, bytes_accessed=12 * 2**20, transcendentals=5 * 10**5
        ),
    )(
        tokens, cotangent, expert_ids.T, slot_index.T, keep_mask.T, route_weight.T,
        w_gate[0], w_up[0], w_down[0],
    )
    out, route, inputs, gate, up, down = pl.pallas_call(
        finish,
        out_shape=tuple(jax.ShapeDtypeStruct(value.shape, value.dtype) for value in results),
        in_specs=[vmem] * 6,
        out_specs=(vmem,) * 6,
        compiler_params=pltpu.CompilerParams(vmem_limit_bytes=60 * 2**20),
    )(*results)
    return out, route.T, inputs, gate.T[None], up.T[None], down[None]


def local_program(*args):
    local, hidden = args[0].shape[0], args[6].shape[2]
    n, groups = lax.axis_size("expert") * args[6].shape[0], lax.axis_size("dp")
    capacity = 5 * local // (2 * n)
    fits = groups == 4 and args[6].shape[0] == 1 and capacity % 8 == 0
    if fits and hidden == 768 and local == 128:
        return fused(*args)
    return body(*args)


def solution(mesh):
    return jax.shard_map(
        local_program,
        mesh=mesh,
        in_specs=(
            P(("expert", "dp"), None),
            P(("expert", "dp"), None),
            P(("expert", "dp"), None),
            P(("expert", "dp"), None),
            P(("expert", "dp"), None),
            P(("expert", "dp"), None),
            P("expert", None, None),
            P("expert", None, None),
            P("expert", None, None),
        ),
        out_specs=(
            P(("expert", "dp"), None),
            P(("expert", "dp"), None),
            P(("expert", "dp"), None),
            P("expert", None, "dp"),
            P("expert", None, "dp"),
            P("expert", "dp", None),
        ),
        check_vma=False,
    )
```
